128 devices in a mesh: grp: 2 (over core), ctx: 64 (over y, z, x).
Axes of the slice: x: 4, y: 4, z: 4, core: 2. Of those that a mesh axis runs over, the one named last changes fastest.
Arguments:
- gla_query: bfloat16 [16384, 4096], P(('grp', 'ctx')), parts along dimension 0, may hold values from -6 to 6
- gla_key: bfloat16 [16384, 4096], P(('grp', 'ctx')), parts along dimension 0, may hold values from -6 to 6
- gla_value: bfloat16 [16384, 4096], P(('grp', 'ctx')), parts along dimension 0, may hold values from -6 to 6
- log_gates: float32 [16384, 32], P(('grp', 'ctx')), parts along dimension 0, may hold values from -1.2 to 0
- norm_gain: float32 [4096], replicated, may hold values from 0.5 to 1.5
- attn_query: bfloat16 [16384, 4096], P(('grp', 'ctx')), parts along dimension 0, may hold values from -6 to 6
- attn_key: bfloat16 [16384, 4096], P(('grp', 'ctx')), parts along dimension 0, may hold values from -4 to 4
- doc_blocks: int32 [16], P('grp'), parts along dimension 0, may hold values from 1 to 32, 64 in all
Outputs:
- gla_mixed: bfloat16 [16384, 4096], P(('grp', 'ctx')), parts along dimension 0
- attended: bfloat16 [16384, 4096], P(('grp', 'ctx')), parts along dimension 0
The draws below stay inside these ranges and needn't reach their ends.
There are 2 independent parts, one for each index of `grp`. The reference program is written for one: setup_inputs(seed, part) draws one part's arguments, and reference() takes and returns one part's arrays. A program takes and returns all parts, laid end to end along the dimension named above; an argument that names none is the same for every part. Nothing has to cross between parts.
Inputs may be any that keep to these rules, and one draw needn't show every extreme that they name: `doc_blocks`: the documents of a group in order, together covering all 8192 tokens; the longest has exactly 32 blocks.
All inputs are finite; a program needn't handle non-finite values.
Results may differ from the reference program's by a relative error of at most 0.0057.
Values may be sent and summed in bfloat16 or wider, within the bound.
A program may use at most 320 MiB of HBM per device.

```python
import math
import jax
import jax.numpy as jnp
import numpy as np
from jax import lax

HEADS = 32
HEAD_DIM = 128
BLOCK = 128
WINDOW = 2048
NDOC = 8
SEGMENT_LENGTH = 8192
BLOCKS = 64
MOSTDOC = 32


def draw_log_gates(key, part):
    subkeys = jax.random.split(jax.random.fold_in(key, 11), 7)
    fast_share = 0.5
    fast_heads = jax.random.uniform(subkeys[0], (HEADS,)) < fast_share
    fast_rates = jnp.exp(jax.random.uniform(subkeys[1], (HEADS,), minval=jnp.log(1.0 / 50.0), maxval=jnp.log(1.0 / 30.0)))
    slow_rates = jax.random.uniform(subkeys[2], (HEADS,), minval=0.05, maxval=0.3) / SEGMENT_LENGTH
    base_rates = jnp.where(fast_heads, fast_rates, slow_rates)
    block_factor = jnp.exp(jax.random.uniform(subkeys[3], (SEGMENT_LENGTH // BLOCK, 1, HEADS), minval=jnp.log(0.6), maxval=jnp.log(1.8)))
    roughness = jax.random.uniform(subkeys[4], (SEGMENT_LENGTH // BLOCK, BLOCK, HEADS), minval=0.5, maxval=1.5)
    forgetting_factors = (base_rates * block_factor * roughness).reshape(SEGMENT_LENGTH, HEADS)
    slot_numbers = jax.random.randint(subkeys[5], (3,), 0, SEGMENT_LENGTH)
    objective_terms = jax.random.uniform(subkeys[6], (3, HEADS), minval=0.2, maxval=0.35)
    segment_ordinal = (jnp.arange(SEGMENT_LENGTH)[:, None] == slot_numbers[None, :]).astype(jnp.float32)
    segment_sequence = jnp.dot(segment_ordinal, jnp.log1p(-objective_terms))
    return (segment_sequence - forgetting_factors).astype(jnp.float32)


def paired(key):
    subkeys = jax.random.split(jax.random.fold_in(key, 23), 2)
    columns = HEADS * HEAD_DIM
    queries = jnp.clip(jax.random.normal(subkeys[0], (SEGMENT_LENGTH, columns)), -4.0, 4.0)
    key_rows = jnp.clip(jax.random.normal(subkeys[1], (SEGMENT_LENGTH, columns)), -4.0, 4.0)
    return (queries, key_rows)


def draw_attn_query(key, part):
    return paired(key)[0].astype(jnp.bfloat16)


def draw_attn_key(key, part):
    return paired(key)[1].astype(jnp.bfloat16)


def block_levels(stream_key, dims, cuts, least, largest):
    level, own = 1.0, jax.random.fold_in(stream_key, 6)
    for position, shards_of in cuts:
        draws = jnp.exp(jax.random.uniform(jax.random.fold_in(own, position), (shards_of,), jnp.float32, least / len(cuts), largest / len(cuts)))
        level = level * jnp.repeat(draws, dims[position] // shards_of).reshape([-1 if axis == position else 1 for axis in range(len(dims))])
    return level


def length_profile(count, total, most, slope):
    portions = [(1 << 20) // math.isqrt(standing ** slope) + 1 for standing in range(2, count + 1)]
    spare, counts = total - most - (count - 1), [1] * (count - 1)
    while spare > 0:
        movable = [i for i in range(count - 1) if counts[i] < most]
        mass, left = sum([portions[i] for i in movable]), spare
        for i in movable:
            addition = min(most - counts[i], max(1, left * portions[i] // mass), spare)
            counts[i] = counts[i] + addition
            spare = spare - addition
    return np.array([most] + counts)


def uneven(own_key, number_of, total, bound, lean):
    if number_of == 2:
        one = jax.random.randint(own_key, (), max(1, total - bound), min(bound, total - 1) + 1)
        return jnp.stack([one, total - one])
    lengths = jnp.asarray(length_profile(number_of, total, bound, lean), jnp.int32)
    couples = (number_of - 1) // 2
    giver, receiver = lengths[1:1 + 2 * couples:2], lengths[2:2 + 2 * couples:2]
    margin = jnp.minimum(giver - 1, bound - receiver)
    shifted = jax.random.randint(jax.random.fold_in(own_key, 1), (couples,), 0, 1 << 20) % (margin + 1)
    lengths = lengths.at[1:1 + 2 * couples:2].set(giver - shifted).at[2:2 + 2 * couples:2].set(receiver + shifted)
    return lengths[jax.random.permutation(jax.random.fold_in(own_key, 2), number_of)]


def gaussian(key, shape, spread, reach, shards=(), held_as=jnp.bfloat16):
    values = jax.random.normal(key, shape, jnp.float32) * spread
    if len(shards) > 0:
        values = block_levels(key, shape, shards, -0.22, 0.18) * values
    return jnp.clip(values, min=-reach, max=reach).astype(held_as)


def setup_inputs(seed: int = 0, part: int = 0) -> dict:
    seeds = jax.random.split(jax.random.key(seed), 9)
    own_keys = jax.random.split(jax.random.fold_in(seeds[8], part), 9)
    gla_query = gaussian(own_keys[0], (SEGMENT_LENGTH, HEADS * HEAD_DIM), 1.0, 6.0, ((0, 64),))
    gla_key = gaussian(own_keys[1], (SEGMENT_LENGTH, HEADS * HEAD_DIM), 1.0, 6.0, ((0, 64),))
    gla_value = gaussian(own_keys[2], (SEGMENT_LENGTH, HEADS * HEAD_DIM), 1.0, 6.0, ((0, 64),))
    log_gates = draw_log_gates(jax.random.fold_in(jax.random.fold_in(seeds[8], part), 71), part)
    norm_gain = jnp.clip(1.0 + 0.1 * jax.random.normal(seeds[4], (HEADS * HEAD_DIM,), jnp.float32), 0.5, 1.5)
    attn_query = draw_attn_query(jax.random.fold_in(jax.random.fold_in(seeds[8], part), 71), part)
    attn_key = draw_attn_key(jax.random.fold_in(jax.random.fold_in(seeds[8], part), 71), part)
    doc_blocks = uneven(own_keys[7], NDOC, BLOCKS, MOSTDOC, 2).astype(jnp.int32)
    return dict(gla_query=gla_query, gla_key=gla_key, gla_value=gla_value, log_gates=log_gates, norm_gain=norm_gain, attn_query=attn_query, attn_key=attn_key, doc_blocks=doc_blocks)


def doc_of_tokens(doc_blocks, total):
    doc_ends = jnp.cumsum(doc_blocks).astype(jnp.int32) * BLOCK
    positions = jnp.arange(total, dtype=jnp.int32)
    return lax.optimization_barrier(jnp.sum((positions[:, None] >= doc_ends[None, :]).astype(jnp.int32), axis=1)).astype(jnp.int32)

def gla_reference(gla_query, gla_key, gla_value, log_gates, norm_gain, doc_blocks):
    total = gla_query.shape[0]
    block_count = total // BLOCK
    doc_ends = jnp.cumsum(doc_blocks).astype(jnp.int32) * BLOCK
    starts = doc_ends - doc_blocks.astype(jnp.int32) * BLOCK
    block_offsets = jnp.arange(block_count, dtype=jnp.int32) * BLOCK
    resets = jnp.any(block_offsets[:, None] == starts[None, :], axis=1).astype(jnp.float32)
    shaped = (block_count, BLOCK, HEADS, HEAD_DIM)
    float_query = gla_query.reshape(shaped).astype(jnp.float32) * HEAD_DIM ** (-0.5)
    float_key = gla_key.reshape(shaped).astype(jnp.float32)
    float_value = gla_value.reshape(shaped).astype(jnp.float32)
    gate_sums = jnp.cumsum(log_gates.reshape(block_count, BLOCK, HEADS), axis=1)
    causal = jnp.arange(BLOCK)[:, None] >= jnp.arange(BLOCK)[None, :]

    def advance(carried, inputs):
        queries, key_rows, value_rows, summed, restart = inputs
        carried = carried * (1.0 - restart)
        block_last = summed[-1]
        by_head = summed.T
        gaps = by_head[:, :, None] - by_head[:, None, :]
        weight = jnp.where(causal[None], jnp.exp(jnp.where(causal[None], gaps, 0.0)), 0.0)
        scores = jnp.einsum('thd,shd->hts', queries, key_rows, precision=lax.Precision.HIGHEST) * weight
        inner_part = jnp.einsum('hts,shd->thd', scores, value_rows, precision=lax.Precision.HIGHEST)
        outer_part = jnp.einsum('thd,hde->the', queries * jnp.exp(summed)[..., None], carried, precision=lax.Precision.HIGHEST)
        tails = jnp.exp(block_last[None, :] - summed)
        updated = jnp.exp(block_last)[:, None, None] * carried + jnp.einsum('shd,she->hde', key_rows * tails[..., None], value_rows, precision=lax.Precision.HIGHEST)
        return (updated, inner_part + outer_part)
    initial = jnp.zeros((HEADS, HEAD_DIM, HEAD_DIM), jnp.float32)
    _, mixture = lax.scan(advance, initial, (float_query, float_key, float_value, gate_sums, resets))
    mean_square = lax.optimization_barrier(jnp.mean(mixture * mixture, axis=-1, keepdims=True))
    rescaled_hidden = mixture * lax.rsqrt(mean_square + 1e-06) * norm_gain.reshape(HEADS, HEAD_DIM)
    return rescaled_hidden.reshape(total, HEADS * HEAD_DIM).astype(jnp.bfloat16)

def attend_reference(queries, key_rows, value_rows, doc_ids):
    total = queries.shape[0]
    tile = min(512, total)

    def by_head(array):
        return array.reshape(total, HEADS, HEAD_DIM).transpose(1, 0, 2)
    pad_docs = jnp.concatenate([jnp.full((WINDOW,), -1, dtype=jnp.int32), doc_ids.astype(jnp.int32)])

    def one_head(operands):
        head_query, head_key, head_value = operands
        pad_key = jnp.concatenate([jnp.zeros((WINDOW, HEAD_DIM), head_key.dtype), head_key])
        pad_value = jnp.concatenate([jnp.zeros((WINDOW, HEAD_DIM), head_value.dtype), head_value])

        def one_tile(tile_index):
            tile_start = (tile_index * tile).astype(jnp.int32)
            tile_rows = lax.dynamic_slice_in_dim(head_query, tile_start, tile, 0)
            key_block = lax.dynamic_slice_in_dim(pad_key, tile_start, WINDOW + tile, 0)
            value_block = lax.dynamic_slice_in_dim(pad_value, tile_start, WINDOW + tile, 0)
            key_docs = lax.dynamic_slice_in_dim(pad_docs, tile_start, WINDOW + tile, 0)
            asker_documents = lax.dynamic_slice_in_dim(doc_ids.astype(jnp.int32), tile_start, tile, 0)
            query_pos = tile_start + jnp.arange(tile, dtype=jnp.int32)
            key_pos = tile_start - WINDOW + jnp.arange(WINDOW + tile, dtype=jnp.int32)
            allowed = (key_pos[None, :] <= query_pos[:, None]) & (key_pos[None, :] > query_pos[:, None] - WINDOW) & (key_docs[None, :] == asker_documents[:, None])
            scores = jnp.dot(tile_rows, key_block.T, preferred_element_type=jnp.float32) * HEAD_DIM ** (-0.5)
            scores = jnp.where(allowed, scores, -1e+30)
            row_peak = lax.optimization_barrier(jnp.max(scores, axis=-1, keepdims=True))
            exponent = jnp.exp(scores - row_peak)
            weights = (exponent / lax.optimization_barrier(jnp.sum(exponent, axis=-1, keepdims=True))).astype(jnp.bfloat16)
            return jnp.dot(weights, value_block, preferred_element_type=jnp.float32).astype(jnp.bfloat16)
        tiles_out = lax.map(one_tile, jnp.arange(total // tile, dtype=jnp.int32))
        return tiles_out.reshape(total, HEAD_DIM)
    result = lax.map(one_head, (by_head(queries), by_head(key_rows), by_head(value_rows)))
    return result.transpose(1, 0, 2).reshape(total, HEADS * HEAD_DIM)

def reference(gla_query, gla_key, gla_value, log_gates, norm_gain, attn_query, attn_key, doc_blocks):
    gla_mixed = gla_reference(gla_query, gla_key, gla_value, log_gates, norm_gain, doc_blocks)
    doc_ids = doc_of_tokens(doc_blocks, gla_query.shape[0])
    attended = attend_reference(attn_query, attn_key, gla_mixed, doc_ids)
    return (gla_mixed, attended)
```

```python
import functools
import math

import jax
import jax.numpy as jnp
from jax import lax
from jax.experimental import pallas as pl
from jax.experimental.pallas import tpu as pltpu
from jax.sharding import PartitionSpec as P

BLOCK = 128
DIM = 128
LOW = -1e30
HIGH = 1e30
SCALE = DIM ** (-0.5)
TO_EXP2 = SCALE / math.log(2.0)
MESH = pl.DeviceIdType.MESH
NT = (((1,), (1,)), ((), ()))
ROWS = DIM + 16


def columns_of(head):
    return pl.ds(pl.multiple_of(head * DIM, DIM), DIM)


def kernel(
    n,
    docs,
    gain,
    gates,
    gla_query,
    gla_key,
    gla_value,
    attn_query,
    attn_key,
    mixed,
    attended,
    gate_out,
    gate_in,
    key_in,
    value_in,
    query_in,
    attn_key_in,
    attn_query_in,
    states,
    decays,
    carry_out,
    carry_in,
    value_t,
    mixed_out,
    attended_out,
    score_t,
    send,
    recv,
    local,
):
    nb = n // 2
    halo = nb // 2
    place = lax.axis_index("ctx")
    half = lax.div(place, nb)
    rank = lax.rem(place, nb)
    base = half * nb
    turn = half * halo
    head = lax.rem(rank + turn, nb)
    partner = (1 - half) * nb + lax.rem(rank + halo, nb)

    lanes = lax.broadcasted_iota(jnp.int32, (BLOCK, BLOCK), 1)
    subs = lax.broadcasted_iota(jnp.int32, (BLOCK, BLOCK), 0)
    wide = jnp.concatenate(
        [gates[...], jnp.zeros((BLOCK, BLOCK - nb), jnp.float32)], axis=1
    )
    upto = jnp.where(subs <= lanes, 1.0, 0.0)
    sums = jnp.dot(
        wide.T, upto, precision=lax.Precision.HIGHEST, preferred_element_type=jnp.float32
    )
    for h in range(nb):
        gate_out[h] = jnp.broadcast_to(sums[h : h + 1], (8, BLOCK))

    barrier = pltpu.get_barrier_semaphore()

    def greet(i, _):
        pl.semaphore_signal(
            barrier, inc=1, device_id={"ctx": lax.rem(place + i, n)}, device_id_type=MESH
        )
        return 0

    lax.fori_loop(1, n, greet, 0)
    pl.semaphore_wait(barrier, n - 1)

    def push(src, dst, which, device):
        pltpu.make_async_remote_copy(
            src_ref=src,
            dst_ref=dst,
            send_sem=send.at[which],
            recv_sem=recv.at[which],
            device_id={"ctx": device},
            device_id_type=MESH,
        ).start()

    def spread(pick, dst, which):
        def one(i, _):
            push(
                pick(lax.rem(head + i, nb)), dst, which, base + lax.rem(rank + i, nb)
            )
            return 0

        lax.fori_loop(1, nb, one, 0)
        pltpu.make_async_copy(pick(head), dst, local.at[which]).start()

    def settle(ref, sem):
        pltpu.make_async_copy(ref, ref, sem).wait()

    def arrive(ref, one, which):
        settle(ref, recv.at[which])
        settle(one, local.at[which])

    def by_columns(src):
        return lambda h: src.at[:, columns_of(h)]

    spread(lambda h: gate_out.at[h], gate_in.at[rank], 0)
    spread(by_columns(gla_key), key_in.at[rank], 1)
    spread(by_columns(gla_value), value_in.at[rank], 2)
    spread(by_columns(gla_query), query_in.at[rank], 3)
    spread(by_columns(attn_key), attn_key_in.at[halo + rank], 4)
    gives_halo = jnp.logical_and(half == 0, rank >= halo)

    @pl.when(gives_halo)
    def _():
        def one(i, _):
            h = lax.rem(head + i, nb)
            push(
                attn_key.at[:, columns_of(h)],
                attn_key_in.at[rank - halo],
                5,
                nb + lax.rem(h + halo, nb),
            )
            return 0

        lax.fori_loop(0, nb, one, 0)

    spread(by_columns(attn_query), attn_query_in.at[rank], 6)

    value_t[:, DIM:, :] = jnp.ones((value_t.shape[0], ROWS - DIM, 2 * BLOCK), jnp.bfloat16)
    carry_zero = jnp.zeros((DIM, DIM), jnp.float32)

    @pl.when(half == 0)
    def _():
        attn_key_in[0:halo] = jnp.zeros((halo, BLOCK, DIM), jnp.bfloat16)
        value_t[0 : halo // 2, 0:DIM, :] = jnp.zeros(
            (halo // 2, DIM, 2 * BLOCK), jnp.bfloat16
        )
        carry_in[...] = carry_zero

    def doc_start(block):
        start = jnp.int32(0)
        best = jnp.int32(0)
        for d in range(docs.shape[0]):
            best = jnp.where(start <= block, start, best)
            start = start + docs[d]
        return best

    arrive(gate_in.at[0 : nb - 1], gate_in.at[0], 0)
    arrive(key_in.at[0 : nb - 1], key_in.at[0], 1)
    arrive(value_in.at[0 : nb - 1], value_in.at[0], 2)

    def gather_states(i, carried):
        state, decay = carried
        for u in range(2):
            b = 2 * i + u
            keep = jnp.where(doc_start(base + b) == base + b, 0.0, 1.0)
            row = gate_in[b][0:1]
            last = row[:, BLOCK - 1 : BLOCK]
            tails = jnp.exp(last - row)
            fade = jnp.exp(last)
            state = state * keep
            decay = decay * keep
            states[b] = state
            decays[b] = decay
            key_t = (key_in[b].astype(jnp.float32).T * tails).astype(jnp.bfloat16)
            state = state * fade + jnp.dot(
                key_t, value_in[b], preferred_element_type=jnp.float32
            )
            decay = decay * fade
        return state, decay

    state, _ = lax.fori_loop(
        0, nb // 2, gather_states, (carry_zero, jnp.ones((8, DIM), jnp.float32))
    )
    carry_out[...] = state

    @pl.when(half == 0)
    def _():
        push(carry_out, carry_in, 7, partner)

    arrive(query_in.at[0 : nb - 1], query_in.at[0], 3)

    @pl.when(half == 1)
    def _():
        settle(carry_in, recv.at[7])

    my_gain = gain[pl.ds(head, 1), :]
    causal = subs >= lanes

    def give_back(src, dst, which, block):
        @pl.when(block != rank)
        def _():
            push(src, dst, which, base + block)

        @pl.when(block == rank)
        def _():
            pltpu.make_async_copy(src, dst, local.at[which]).start()

    def mix(i, _):
        for u in range(2):
            b = 2 * i + u
            query = query_in[b]
            value = value_in[b]
            across = jnp.broadcast_to(gate_in[b][0:1], (BLOCK, BLOCK))
            down = across.T
            weight = jnp.where(
                causal, jnp.exp(jnp.where(causal, down - across, 0.0)), 0.0
            )
            scores = lax.dot_general(
                query, key_in[b], NT, preferred_element_type=jnp.float32
            )
            inner = jnp.dot(
                (scores * (weight * SCALE)).astype(jnp.bfloat16),
                value,
                preferred_element_type=jnp.float32,
            )
            entering = states[b] + decays[b][0:1] * carry_in[...]
            outer = jnp.dot(
                query, entering.astype(jnp.bfloat16), preferred_element_type=jnp.float32
            )
            total = inner + (jnp.exp(down) * SCALE) * outer
            square = jnp.mean(total * total, axis=-1, keepdims=True)
            result = total * lax.rsqrt(square + 1e-06) * my_gain
            mixed_out[b] = result.astype(jnp.bfloat16)
            value_t[halo // 2 + i, 0:DIM, u * BLOCK : (u + 1) * BLOCK] = result.T.astype(
                jnp.bfloat16
            )
            give_back(mixed_out.at[b], mixed.at[:, columns_of(head)], 8, b)

        @pl.when(jnp.logical_and(half == 0, i >= halo // 2))
        def _():
            push(
                value_t.at[halo // 2 + i, 0:DIM, :],
                value_t.at[i - halo // 2, 0:DIM, :],
                9,
                partner,
            )

        return 0

    lax.fori_loop(0, nb // 2, mix, 0)

    arrive(attn_key_in.at[halo : halo + nb - 1], attn_key_in.at[halo], 4)
    arrive(attn_query_in.at[0 : nb - 1], attn_query_in.at[0], 6)

    @pl.when(half == 1)
    def _():
        settle(attn_key_in.at[0:halo], recv.at[5])
        settle(value_t.at[0 : halo // 2, 0:DIM, :], recv.at[9])

    tile = 2 * BLOCK
    steps = halo // 2 + 1
    tile_lanes = lax.broadcasted_iota(jnp.int32, (tile, tile), 1)
    tile_subs = lax.broadcasted_iota(jnp.int32, (tile, tile), 0)
    first_lanes = lax.broadcasted_iota(jnp.int32, (8, tile), 1) < BLOCK

    def attend(i, _):
        query = attn_query_in[pl.ds(2 * i, 2)].reshape(tile, DIM)
        first = base + 2 * i
        start = jnp.where(first_lanes, doc_start(first), doc_start(first + 1))
        peak = jnp.full((8, tile), LOW, jnp.float32)
        for j in range(steps):
            keys = attn_key_in[pl.ds(2 * (i + j), 2)].reshape(tile, DIM)
            scores = lax.dot_general(keys, query, NT, preferred_element_type=jnp.float32)
            if j == 0:
                scores = jnp.where(tile_subs > tile_lanes, scores, LOW)
            if j == steps - 1:
                scores = jnp.where(tile_subs <= tile_lanes, scores, LOW)
            score_t[j] = scores
            for u in range(2):
                block = first - halo + 2 * j + u
                top = jnp.max(
                    scores[u * BLOCK : (u + 1) * BLOCK].reshape(BLOCK // 8, 8, tile), axis=0
                )
                peak = jnp.maximum(peak, jnp.where(start <= block, top, LOW))
        peak = jnp.max(peak, axis=0, keepdims=True)
        total = jnp.zeros((ROWS, tile), jnp.float32)
        for j in range(steps):
            parts = []
            for u in range(2):
                block = first - halo + 2 * j + u
                level = jnp.where(start[0:1] <= block, peak, HIGH)
                part = score_t[j, u * BLOCK : (u + 1) * BLOCK, :]
                parts.append(jnp.exp2((part - level) * TO_EXP2).astype(jnp.bfloat16))
            total = total + jnp.dot(
                value_t[i + j],
                jnp.concatenate(parts, axis=0),
                preferred_element_type=jnp.float32,
            )
        result = (total[0:DIM] / total[DIM : DIM + 1]).T.astype(jnp.bfloat16)
        for u in range(2):
            b = 2 * i + u
            attended_out[b] = result[u * BLOCK : (u + 1) * BLOCK]
            give_back(attended_out.at[b], attended.at[:, columns_of(head)], 10, b)
        return 0

    lax.fori_loop(0, nb // 2, attend, 0)

    most = columns_of(0)
    most = pl.ds(0, (nb - 1) * DIM)
    for which, out in ((8, mixed), (10, attended)):
        settle(out.at[:, most], recv.at[which])
        settle(out.at[:, columns_of(0)], local.at[which])
    settle(gate_out.at[0 : nb - 1], send.at[0])
    for which in (1, 2, 3, 4, 6, 8, 10):
        settle(key_in.at[0 : nb - 1], send.at[which])

    @pl.when(gives_halo)
    def _():
        settle(key_in.at[0:nb], send.at[5])

    @pl.when(half == 0)
    def _():
        settle(carry_out, send.at[7])
        settle(value_t.at[0 : halo // 2, 0:DIM, :], send.at[9])


def body(gla_query, gla_key, gla_value, log_gates, norm_gain, attn_query, attn_key, doc_blocks):
    n = lax.axis_size("ctx")
    nb = n // 2
    halo = nb // 2
    rows, columns = gla_query.shape
    out = jax.ShapeDtypeStruct((rows, columns), jnp.bfloat16)
    anywhere = pl.BlockSpec(memory_space=pl.ANY)
    vmem = pl.BlockSpec(memory_space=pltpu.VMEM)
    f32, bf16 = jnp.float32, jnp.bfloat16
    return pl.pallas_call(
        functools.partial(kernel, n),
        out_shape=(out, out),
        in_specs=[pl.BlockSpec(memory_space=pltpu.SMEM), vmem, vmem] + [anywhere] * 5,
        out_specs=(anywhere, anywhere),
        scratch_shapes=[
            pltpu.VMEM((nb, 8, BLOCK), f32),
            pltpu.VMEM((nb, 8, BLOCK), f32),
            pltpu.VMEM((nb, BLOCK, DIM), bf16),
            pltpu.VMEM((nb, BLOCK, DIM), bf16),
            pltpu.VMEM((nb, BLOCK, DIM), bf16),
            pltpu.VMEM((halo + nb, BLOCK, DIM), bf16),
            pltpu.VMEM((nb, BLOCK, DIM), bf16),
            pltpu.VMEM((nb, DIM, DIM), f32),
            pltpu.VMEM((nb, 8, DIM), f32),
            pltpu.VMEM((DIM, DIM), f32),
            pltpu.VMEM((DIM, DIM), f32),
            pltpu.VMEM(((halo + nb) // 2, ROWS, 2 * BLOCK), bf16),
            pltpu.VMEM((nb, BLOCK, DIM), bf16),
            pltpu.VMEM((nb, BLOCK, DIM), bf16),
            pltpu.VMEM((halo // 2 + 1, 2 * BLOCK, 2 * BLOCK), f32),
            pltpu.SemaphoreType.DMA((11,)),
            pltpu.SemaphoreType.DMA((11,)),
            pltpu.SemaphoreType.DMA((11,)),
        ],
        compiler_params=pltpu.CompilerParams(
            collective_id=0, has_side_effects=True, vmem_limit_bytes=40 * 2**20
        ),
    )(
        doc_blocks,
        norm_gain.reshape(nb, DIM),
        log_gates,
        gla_query,
        gla_key,
        gla_value,
        attn_query,
        attn_key,
    )


def solution(mesh):
    placed = P(("grp", "ctx"), None)
    return jax.shard_map(
        body,
        mesh=mesh,
        in_specs=(placed, placed, placed, placed, P(), placed, placed, P("grp")),
        out_specs=(placed, placed),
        check_vma=False,
    )
```

```python
import functools
import math

import jax
import jax.numpy as jnp
from jax import lax
from jax.experimental import pallas as pl
from jax.experimental.pallas import tpu as pltpu
from jax.sharding import PartitionSpec as P

BLOCK = 128
DIM = 128
LOW = -1e30
HIGH = 1e30
SCALE = DIM ** (-0.5)
TO_EXP2 = SCALE / math.log(2.0)
MESH = pl.DeviceIdType.MESH
NT = (((1,), (1,)), ((), ()))
ROWS = DIM + 16


def columns_of(head):
    return pl.ds(pl.multiple_of(head * DIM, DIM), DIM)


def kernel(
    n,
    docs,
    gain,
    gates,
    gla_query,
    gla_key,
    gla_value,
    attn_query,
    attn_key,
    mixed,
    attended,
    own_query,
    own_key,
    own_value,
    sums,
    fade_out,
    fade_in,
    state_out,
    state_in,
    entering_out,
    entering_in,
    inner,
    mixed_out,
    value_out,
    value_t,
    attn_key_in,
    attn_query_in,
    score_t,
    weights_t,
    attended_out,
    send,
    recv,
    local,
):
    nb = n // 2
    halo = nb // 2
    part = DIM // 2
    place = lax.axis_index("ctx")
    half = lax.div(place, nb)
    rank = lax.rem(place, nb)
    base = half * nb
    turn = half * halo
    head = lax.rem(rank + turn, nb)
    partner = (1 - half) * nb + lax.rem(rank + halo, nb)
    barrier = pltpu.get_barrier_semaphore()

    def greet(i, _):
        pl.semaphore_signal(
            barrier, inc=1, device_id={"ctx": lax.rem(place + i, n)}, device_id_type=MESH
        )
        return 0

    lax.fori_loop(1, n, greet, 0)

    def push(src, dst, which, device):
        pltpu.make_async_remote_copy(
            src_ref=src,
            dst_ref=dst,
            send_sem=send.at[which],
            recv_sem=recv.at[which],
            device_id={"ctx": device},
            device_id_type=MESH,
        ).start()

    def push_any(src, dst, which, device):
        @pl.when(device != place)
        def _():
            push(src, dst, which, device)

        @pl.when(device == place)
        def _():
            pltpu.make_async_copy(src, dst, local.at[which]).start()

    def settle(ref, sem):
        pltpu.make_async_copy(ref, ref, sem).wait()

    def arrive(ref, one, which):
        settle(ref, recv.at[which])
        settle(one, local.at[which])

    pltpu.make_async_copy(gla_key, own_key, local.at[9]).start()
    pltpu.make_async_copy(gla_value, own_value, local.at[10]).start()
    pltpu.make_async_copy(gla_query, own_query, local.at[11]).start()

    lanes = lax.broadcasted_iota(jnp.int32, (BLOCK, BLOCK), 1)
    subs = lax.broadcasted_iota(jnp.int32, (BLOCK, BLOCK), 0)
    upto = jnp.where(subs <= lanes, 1.0, 0.0)
    summed = jnp.dot(
        gates[...], upto, precision=lax.Precision.HIGHEST, preferred_element_type=jnp.float32
    )
    for h in range(nb):
        sums[h] = summed[h : h + 1]
        fade_out[h] = jnp.exp(jnp.broadcast_to(summed[h : h + 1, BLOCK - 1 :], (1, BLOCK)))
    value_t[:, DIM:, :] = jnp.ones((value_t.shape[0], ROWS - DIM, BLOCK), jnp.bfloat16)

    @pl.when(half == 0)
    def _():
        attn_key_in[0:halo] = jnp.zeros((halo, BLOCK, DIM), jnp.bfloat16)
        value_t[0:halo, 0:DIM, :] = jnp.zeros((halo, DIM, BLOCK), jnp.bfloat16)

    def doc_start(block):
        start = jnp.int32(0)
        best = jnp.int32(0)
        for d in range(docs.shape[0]):
            best = jnp.where(start <= block, start, best)
            start = start + docs[d]
        return best

    settle(own_key, local.at[9])
    settle(own_value, local.at[10])
    pl.semaphore_wait(barrier, n - 1)

    def gained(i, _):
        for u in range(2):
            h = lax.rem(rank + 2 * i + u, nb)
            row = sums[h]
            tails = jnp.exp(row[:, BLOCK - 1 :] - row)
            key_t = own_key[:, columns_of(h)].astype(jnp.float32).T * tails
            state = jnp.dot(
                key_t.astype(jnp.bfloat16),
                own_value[:, columns_of(h)],
                preferred_element_type=jnp.float32,
            )
            state_out[h] = state.astype(jnp.bfloat16)
            for w in range(2):
                owner = h + w * nb
                push_any(fade_out.at[h], fade_in.at[place], 0, owner)
                push_any(
                    state_out.at[h, w * part : (w + 1) * part], state_in.at[place], 1, owner
                )
        return 0

    lax.fori_loop(0, nb // 2, gained, 0)

    def spread(src, dst, which):
        def one(i, _):
            h = lax.rem(head + i, nb)
            push(src.at[:, columns_of(h)], dst, which, base + lax.rem(rank + i, nb))
            return 0

        lax.fori_loop(1, nb, one, 0)
        pltpu.make_async_copy(src.at[:, columns_of(head)], dst, local.at[which]).start()

    spread(attn_key, attn_key_in.at[halo + rank], 2)
    settle(own_query, local.at[11])
    causal = subs >= lanes

    def within(i, _):
        for u in range(2):
            h = 2 * i + u
            across = jnp.broadcast_to(sums[h], (BLOCK, BLOCK))
            down = across.T
            weight = jnp.where(
                causal, jnp.exp(jnp.where(causal, down - across, 0.0)), 0.0
            )
            scores = lax.dot_general(
                own_query[:, columns_of(h)],
                own_key[:, columns_of(h)],
                NT,
                preferred_element_type=jnp.float32,
            )
            inner[h] = jnp.dot(
                (scores * (weight * SCALE)).astype(jnp.bfloat16),
                own_value[:, columns_of(h)],
                preferred_element_type=jnp.float32,
            )
        return 0

    lax.fori_loop(0, nb // 2, within, 0)

    arrive(fade_in.at[0 : n - 1], fade_in.at[0], 0)
    arrive(state_in.at[0 : n - 1], state_in.at[0], 1)

    def scan(i, state):
        for u in range(2):
            b = 2 * i + u
            state = state * jnp.where(doc_start(b) == b, 0.0, 1.0)
            entering_out[b] = state.astype(jnp.bfloat16)
            state = state * fade_in[b] + state_in[b].astype(jnp.float32)
        return state

    lax.fori_loop(0, nb, scan, jnp.zeros((part, DIM), jnp.float32))

    mine = entering_in.at[2 * rank + half]

    def enter(i, _):
        device = lax.rem(place + i, n)
        push(entering_out.at[device], mine, 3, device)
        return 0

    lax.fori_loop(1, n, enter, 0)
    pltpu.make_async_copy(entering_out.at[place], mine, local.at[3]).start()

    spread(attn_query, attn_query_in.at[rank], 4)
    arrive(attn_key_in.at[halo : halo + nb - 1], attn_key_in.at[halo], 2)

    @pl.when(half == 0)
    def _():
        push(attn_key_in.at[nb : nb + halo], attn_key_in.at[0:halo], 5, partner)

    arrive(entering_in.at[0 : n - 1], entering_in.at[0], 3)

    def mix(i, _):
        for u in range(2):
            h = lax.rem(head + 2 * i + u, nb)
            down = jnp.broadcast_to(sums[h], (BLOCK, BLOCK)).T
            entering = entering_in[pl.ds(2 * h, 2)].reshape(DIM, DIM)
            outer = jnp.dot(
                own_query[:, columns_of(h)], entering, preferred_element_type=jnp.float32
            )
            total = inner[h] + (jnp.exp(down) * SCALE) * outer
            square = jnp.mean(total * total, axis=-1, keepdims=True)
            result = total * lax.rsqrt(square + 1e-06) * gain[pl.ds(h, 1), :]
            value_out[h] = result.T.astype(jnp.bfloat16)
            push_any(
                value_out.at[h],
                value_t.at[halo + rank, 0:DIM],
                6,
                base + lax.rem(h + turn, nb),
            )
            mixed_out[h] = result.astype(jnp.bfloat16)
            pltpu.make_async_copy(
                mixed_out.at[h], mixed.at[:, columns_of(h)], local.at[9]
            ).start()
        return 0

    lax.fori_loop(0, nb // 2, mix, 0)

    arrive(attn_query_in.at[0 : nb - 1], attn_query_in.at[0], 4)

    @pl.when(half == 1)
    def _():
        settle(attn_key_in.at[0:halo], recv.at[5])

    tile = 2 * BLOCK
    tiles = nb // 2
    steps = halo // 2 + 1
    tile_lanes = lax.broadcasted_iota(jnp.int32, (tile, tile), 1)
    tile_subs = lax.broadcasted_iota(jnp.int32, (tile, tile), 0)
    first_lanes = lax.broadcasted_iota(jnp.int32, (8, tile), 1) < BLOCK

    def weigh(i, _):
        query = attn_query_in[pl.ds(2 * i, 2)].reshape(tile, DIM)
        first = base + 2 * i
        start = jnp.where(first_lanes, doc_start(first), doc_start(first + 1))
        peak = jnp.full((8, tile), LOW, jnp.float32)
        for j in range(steps):
            keys = attn_key_in[pl.ds(2 * (i + j), 2)].reshape(tile, DIM)
            scores = lax.dot_general(keys, query, NT, preferred_element_type=jnp.float32)
            if j == 0:
                scores = jnp.where(tile_subs > tile_lanes, scores, LOW)
            if j == steps - 1:
                scores = jnp.where(tile_subs <= tile_lanes, scores, LOW)
            score_t[j] = scores
            for u in range(2):
                block = first - halo + 2 * j + u
                top = jnp.max(
                    scores[u * BLOCK : (u + 1) * BLOCK].reshape(BLOCK // 8, 8, tile), axis=0
                )
                peak = jnp.maximum(peak, jnp.where(start <= block, top, LOW))
        peak = jnp.max(peak, axis=0, keepdims=True)
        for j in range(steps):
            for u in range(2):
                block = first - halo + 2 * j + u
                level = jnp.where(start[0:1] <= block, peak, HIGH)
                span = slice(u * BLOCK, (u + 1) * BLOCK)
                weights_t[i, j, span, :] = jnp.exp2(
                    (score_t[j, span, :] - level) * TO_EXP2
                ).astype(jnp.bfloat16)
        return 0

    lax.fori_loop(0, tiles, weigh, 0)

    arrive(value_t.at[halo : halo + nb - 1, 0:DIM], value_t.at[halo, 0:DIM], 6)

    @pl.when(half == 0)
    def _():
        push(value_t.at[nb : nb + halo, 0:DIM], value_t.at[0:halo, 0:DIM], 7, partner)

    def attend(i, _):
        total = jnp.zeros((ROWS, tile), jnp.float32)
        for j in range(steps):
            at = 2 * (i + j)
            total = total + jnp.dot(
                jnp.concatenate([value_t[at], value_t[at + 1]], axis=1),
                weights_t[i, j],
                preferred_element_type=jnp.float32,
            )
        result = (total[0:DIM] / total[DIM : DIM + 1]).T.astype(jnp.bfloat16)
        for u in range(2):
            b = 2 * i + u
            attended_out[b] = result[u * BLOCK : (u + 1) * BLOCK]
            push_any(attended_out.at[b], attended.at[:, columns_of(head)], 8, base + b)
        return 0

    lax.fori_loop(tiles // 2, tiles, attend, 0)

    @pl.when(half == 1)
    def _():
        settle(value_t.at[0:halo, 0:DIM], recv.at[7])

    lax.fori_loop(0, tiles // 2, attend, 0)

    settle(mixed, local.at[9])
    arrive(attended.at[:, pl.ds(0, (nb - 1) * DIM)], attended.at[:, columns_of(0)], 8)
    settle(fade_in.at[0 : n - 1], send.at[0])
    settle(state_in.at[0 : n - 1], send.at[1])
    settle(entering_in.at[0 : n - 1], send.at[3])
    for which in (2, 4, 6, 8):
        settle(value_out.at[0 : nb - 1], send.at[which])

    @pl.when(half == 0)
    def _():
        settle(value_out.at[0:halo], send.at[5])
        settle(value_out.at[0:halo], send.at[7])


def body(gla_query, gla_key, gla_value, log_gates, norm_gain, attn_query, attn_key, doc_blocks):
    n = lax.axis_size("ctx")
    nb = n // 2
    halo = nb // 2
    rows, columns = gla_query.shape
    out = jax.ShapeDtypeStruct((rows, columns), jnp.bfloat16)
    anywhere = pl.BlockSpec(memory_space=pl.ANY)
    vmem = pl.BlockSpec(memory_space=pltpu.VMEM)
    f32, bf16 = jnp.float32, jnp.bfloat16
    square = (BLOCK, DIM)
    tile = 2 * BLOCK
    steps = halo // 2 + 1
    return pl.pallas_call(
        functools.partial(kernel, n),
        out_shape=(out, out),
        in_specs=[pl.BlockSpec(memory_space=pltpu.SMEM), vmem, vmem] + [anywhere] * 5,
        out_specs=(anywhere, anywhere),
        scratch_shapes=[
            pltpu.VMEM((rows, columns), bf16),
            pltpu.VMEM((rows, columns), bf16),
            pltpu.VMEM((rows, columns), bf16),
            pltpu.VMEM((nb, 1, BLOCK), f32),
            pltpu.VMEM((nb, 1, BLOCK), f32),
            pltpu.VMEM((n, 1, BLOCK), f32),
            pltpu.VMEM((nb, DIM, DIM), bf16),
            pltpu.VMEM((n, DIM // 2, DIM), bf16),
            pltpu.VMEM((n, DIM // 2, DIM), bf16),
            pltpu.VMEM((n, DIM // 2, DIM), bf16),
            pltpu.VMEM((nb, *square), f32),
            pltpu.VMEM((nb, *square), bf16),
            pltpu.VMEM((nb, *square), bf16),
            pltpu.VMEM((halo + nb, ROWS, BLOCK), bf16),
            pltpu.VMEM((halo + nb, *square), bf16),
            pltpu.VMEM((nb, *square), bf16),
            pltpu.VMEM((steps, tile, tile), f32),
            pltpu.VMEM((nb // 2, steps, tile, tile), bf16),
            pltpu.VMEM((nb, *square), bf16),
            pltpu.SemaphoreType.DMA((12,)),
            pltpu.SemaphoreType.DMA((12,)),
            pltpu.SemaphoreType.DMA((12,)),
        ],
        compiler_params=pltpu.CompilerParams(
            collective_id=0, has_side_effects=True, vmem_limit_bytes=60 * 2**20
        ),
    )(
        doc_blocks,
        norm_gain.reshape(nb, DIM),
        log_gates.T,
        gla_query,
        gla_key,
        gla_value,
        attn_query,
        attn_key,
    )


def solution(mesh):
    placed = P(("grp", "ctx"), None)
    return jax.shard_map(
        body,
        mesh=mesh,
        in_specs=(placed, placed, placed, placed, P(), placed, placed, P("grp")),
        out_specs=(placed, placed),
        check_vma=False,
    )
```

```python
import functools
import math

import jax
import jax.numpy as jnp
from jax import lax
from jax.experimental import pallas as pl
from jax.experimental.pallas import tpu as pltpu
from jax.sharding import PartitionSpec as P

BLOCK = 128
DIM = 128
LOW = -1e30
HIGH = 1e30
SCALE = DIM ** (-0.5)
TO_EXP2 = SCALE / math.log(2.0)
MESH = pl.DeviceIdType.MESH
NT = (((1,), (1,)), ((), ()))
ROWS = DIM + 16
STRIDE = 5
EARLY = 8


def columns_of(head):
    return pl.ds(pl.multiple_of(head * DIM, DIM), DIM)


def kernel(
    n,
    docs,
    gain,
    gates,
    gla_query,
    gla_key,
    gla_value,
    attn_query,
    attn_key,
    mixed,
    attended,
    own_query,
    own_key,
    own_value,
    own_value_t,
    gain_t,
    sums,
    fade_out,
    fade_in,
    state_out,
    state_in,
    entering_out,
    entering_in,
    inner,
    mixed_out,
    value_out,
    value_t,
    attn_key_in,
    attn_query_in,
    score_t,
    weights_t,
    attended_out,
    send,
    recv,
    local,
    recv_value,
):
    nb = n // 2
    halo = nb // 2
    part = DIM // 2
    place = lax.axis_index("ctx")
    half = lax.div(place, nb)
    rank = lax.rem(place, nb)
    base = half * nb
    turn = half * halo
    head = lax.rem(rank + turn, nb)
    partner = (1 - half) * nb + lax.rem(rank + halo, nb)
    barrier = pltpu.get_barrier_semaphore()

    def greet(i, _):
        pl.semaphore_signal(
            barrier, inc=1, device_id={"ctx": lax.rem(place + i, n)}, device_id_type=MESH
        )
        return 0

    lax.fori_loop(1, n, greet, 0)

    def push(src, dst, which, device):
        pltpu.make_async_remote_copy(
            src_ref=src,
            dst_ref=dst,
            send_sem=send.at[which],
            recv_sem=recv.at[which],
            device_id={"ctx": device},
            device_id_type=MESH,
        ).start()

    def push_any(src, dst, which, device):
        @pl.when(device != place)
        def _():
            push(src, dst, which, device)

        @pl.when(device == place)
        def _():
            pltpu.make_async_copy(src, dst, local.at[which]).start()

    def settle(ref, sem):
        pltpu.make_async_copy(ref, ref, sem).wait()

    def arrive(ref, one, which):
        settle(ref, recv.at[which])
        settle(one, local.at[which])

    pltpu.make_async_copy(gla_key, own_key, local.at[9]).start()
    pltpu.make_async_copy(gla_value, own_value, local.at[10]).start()
    pltpu.make_async_copy(gla_query, own_query, local.at[11]).start()

    pl.semaphore_wait(barrier, n - 1)

    def spread(src, dst, which):
        def one(i, _):
            h = lax.rem(head + STRIDE * i, nb)
            push(src.at[:, columns_of(h)], dst, which, base + lax.rem(rank + STRIDE * i, nb))
            return 0

        lax.fori_loop(1, nb, one, 0)
        pltpu.make_async_copy(src.at[:, columns_of(head)], dst, local.at[which]).start()

    spread(attn_key, attn_key_in.at[halo + rank], 2)

    lanes = lax.broadcasted_iota(jnp.int32, (BLOCK, BLOCK), 1)
    subs = lax.broadcasted_iota(jnp.int32, (BLOCK, BLOCK), 0)
    upto = jnp.where(subs <= lanes, 1.0, 0.0)
    summed = jnp.dot(
        gates[...], upto, precision=lax.Precision.HIGHEST, preferred_element_type=jnp.float32
    )
    for h in range(nb):
        sums[h] = summed[h : h + 1]
        fade_out[h] = jnp.exp(jnp.broadcast_to(summed[h : h + 1, BLOCK - 1 :], (1, BLOCK)))
    value_t[:, DIM:, :] = jnp.ones((value_t.shape[0], ROWS - DIM, BLOCK), jnp.bfloat16)

    @pl.when(half == 0)
    def _():
        attn_key_in[0:halo] = jnp.zeros((halo, BLOCK, DIM), jnp.bfloat16)
        value_t[0:halo, 0:DIM, :] = jnp.zeros((halo, DIM, BLOCK), jnp.bfloat16)

    def doc_start(block):
        start = jnp.int32(0)
        best = jnp.int32(0)
        for d in range(docs.shape[0]):
            best = jnp.where(start <= block, start, best)
            start = start + docs[d]
        return best

    settle(own_key, local.at[9])
    settle(own_value, local.at[10])

    def gained(i, _):
        for u in range(2):
            h = lax.rem(rank + STRIDE * (2 * i + u), nb)
            row = sums[h]
            tails = jnp.exp(row[:, BLOCK - 1 :] - row)
            turned = own_value[:, columns_of(h)].astype(jnp.float32).T
            own_value_t[h] = turned.astype(jnp.bfloat16)
            state = jnp.dot(
                (turned * tails).astype(jnp.bfloat16),
                own_key[:, columns_of(h)],
                preferred_element_type=jnp.float32,
            )
            state_out[h] = state.astype(jnp.bfloat16)
            for w in range(2):
                owner = h + w * nb
                push_any(fade_out.at[h], fade_in.at[place], 0, owner)
                push_any(
                    state_out.at[h, w * part : (w + 1) * part], state_in.at[place], 1, owner
                )
        return 0

    lax.fori_loop(0, nb // 2, gained, 0)

    spread(attn_query, attn_query_in.at[rank], 4)
    settle(own_query, local.at[11])
    causal = subs >= lanes

    def within(i, _):
        for u in range(2):
            h = 2 * i + u
            across = jnp.broadcast_to(sums[h], (BLOCK, BLOCK))
            down = across.T
            weight = jnp.where(
                causal, jnp.exp(jnp.where(causal, down - across, 0.0)), 0.0
            )
            scores = lax.dot_general(
                own_query[:, columns_of(h)],
                own_key[:, columns_of(h)],
                NT,
                preferred_element_type=jnp.float32,
            )
            inner[h] = lax.dot_general(
                own_value_t[h],
                (scores * (weight * SCALE)).astype(jnp.bfloat16),
                NT,
                preferred_element_type=jnp.float32,
            )
            gain_t[h] = jnp.broadcast_to(gain[pl.ds(h, 1), :], (BLOCK, DIM)).T
        return 0

    lax.fori_loop(0, nb // 2, within, 0)
    arrive(attn_key_in.at[halo : halo + nb - 1], attn_key_in.at[halo], 2)

    @pl.when(half == 0)
    def _():
        push(attn_key_in.at[nb : nb + halo], attn_key_in.at[0:halo], 5, partner)


    arrive(fade_in.at[0 : n - 1], fade_in.at[0], 0)
    arrive(state_in.at[0 : n - 1], state_in.at[0], 1)

    def scan(i, state):
        for u in range(2):
            b = 2 * i + u
            state = state * jnp.where(doc_start(b) == b, 0.0, 1.0)
            entering_out[b] = state.astype(jnp.bfloat16)
            state = state * fade_in[b] + state_in[b].astype(jnp.float32)
        return state

    lax.fori_loop(0, nb, scan, jnp.zeros((part, DIM), jnp.float32))

    mine = entering_in.at[2 * rank + half]

    def enter(i, _):
        device = lax.rem(place + STRIDE * i, n)
        push(entering_out.at[device], mine, 3, device)
        return 0

    lax.fori_loop(1, n, enter, 0)
    pltpu.make_async_copy(entering_out.at[place], mine, local.at[3]).start()

    arrive(attn_query_in.at[0 : nb - 1], attn_query_in.at[0], 4)

    tile = 2 * BLOCK
    tiles = nb // 2
    steps = halo // 2 + 1
    tile_lanes = lax.broadcasted_iota(jnp.int32, (tile, tile), 1)
    tile_subs = lax.broadcasted_iota(jnp.int32, (tile, tile), 0)
    first_lanes = lax.broadcasted_iota(jnp.int32, (8, tile), 1) < BLOCK

    def weigh(k, _):
        i = lax.rem(k + tiles // 2, tiles)
        query = attn_query_in[pl.ds(2 * i, 2)].reshape(tile, DIM)
        first = base + 2 * i
        start = jnp.where(first_lanes, doc_start(first), doc_start(first + 1))
        peak = jnp.full((8, tile), LOW, jnp.float32)
        for j in range(steps):
            keys = attn_key_in[pl.ds(2 * (i + j), 2)].reshape(tile, DIM)
            scores = lax.dot_general(keys, query, NT, preferred_element_type=jnp.float32)
            if j == 0:
                scores = jnp.where(tile_subs > tile_lanes, scores, LOW)
            if j == steps - 1:
                scores = jnp.where(tile_subs <= tile_lanes, scores, LOW)
            score_t[j] = scores
            for u in range(2):
                block = first - halo + 2 * j + u
                top = jnp.max(
                    scores[u * BLOCK : (u + 1) * BLOCK].reshape(BLOCK // 8, 8, tile), axis=0
                )
                peak = jnp.maximum(peak, jnp.where(start <= block, top, LOW))
        peak = jnp.max(peak, axis=0, keepdims=True)
        for j in range(steps):
            for u in range(2):
                block = first - halo + 2 * j + u
                level = jnp.where(start[0:1] <= block, peak, HIGH)
                span = slice(u * BLOCK, (u + 1) * BLOCK)
                weights_t[i, j, span, :] = jnp.exp2(
                    (score_t[j, span, :] - level) * TO_EXP2
                ).astype(jnp.bfloat16)
        return 0

    lax.fori_loop(0, EARLY, weigh, 0)
    arrive(entering_in.at[0 : n - 1], entering_in.at[0], 3)

    def mix(i, _):
        for u in range(2):
            h = lax.rem(head + STRIDE * (2 * i + u), nb)
            entering = entering_in[pl.ds(2 * h, 2)].reshape(DIM, DIM)
            outer = lax.dot_general(
                entering,
                own_query[:, columns_of(h)],
                NT,
                preferred_element_type=jnp.float32,
            )
            total = inner[h] + (jnp.exp(sums[h]) * SCALE) * outer
            square = jnp.mean(total * total, axis=0, keepdims=True)
            value_out[h] = (total * lax.rsqrt(square + 1e-06) * gain_t[h]).astype(
                jnp.bfloat16
            )
            device = base + lax.rem(h + turn, nb)
            block = value_t.at[halo + rank, 0:DIM]

            @pl.when(device != place)
            def _():
                pltpu.make_async_remote_copy(
                    src_ref=value_out.at[h],
                    dst_ref=block,
                    send_sem=send.at[6],
                    recv_sem=recv_value.at[rank],
                    device_id={"ctx": device},
                    device_id_type=MESH,
                ).start()

            @pl.when(device == place)
            def _():
                pltpu.make_async_copy(value_out.at[h], block, local.at[6]).start()

        return 0

    lax.fori_loop(0, nb // 2, mix, 0)

    @pl.when(half == 1)
    def _():
        settle(attn_key_in.at[0:halo], recv.at[5])

    late = tiles - EARLY
    per_tile = nb // late

    def take(i):
        source = lax.rem(rank + nb - lax.rem(STRIDE * i, nb), nb)
        block = value_t.at[halo + source, 0:DIM]

        @pl.when(i == 0)
        def _():
            settle(block, local.at[6])

        @pl.when(i > 0)
        def _():
            settle(block, recv_value.at[source])

        @pl.when(jnp.logical_and(half == 0, source >= halo))
        def _():
            pltpu.make_async_remote_copy(
                src_ref=block,
                dst_ref=value_t.at[source - halo, 0:DIM],
                send_sem=send.at[7],
                recv_sem=recv.at[7],
                device_id={"ctx": partner},
                device_id_type=MESH,
            ).start()

    def weigh_and_take(k, _):
        weigh(EARLY + k, 0)
        for u in range(per_tile):
            h = k * per_tile + u
            mixed_out[h] = value_out[h].T
            pltpu.make_async_copy(
                mixed_out.at[h], mixed.at[:, columns_of(h)], local.at[9]
            ).start()
            take(h)
        return 0

    lax.fori_loop(0, late, weigh_and_take, 0)

    def attend(k, _):
        i = lax.div(k, tiles // 2) * (tiles // 2) + lax.rem(k + rank, tiles // 2)
        total = jnp.zeros((ROWS, tile), jnp.float32)
        for j in range(steps):
            at = 2 * (i + j)
            total = total + jnp.dot(
                jnp.concatenate([value_t[at], value_t[at + 1]], axis=1),
                weights_t[i, j],
                preferred_element_type=jnp.float32,
            )
        result = (total[0:DIM] / total[DIM : DIM + 1]).T.astype(jnp.bfloat16)
        for u in range(2):
            b = 2 * i + u
            attended_out[b] = result[u * BLOCK : (u + 1) * BLOCK]
            push_any(attended_out.at[b], attended.at[:, columns_of(head)], 8, base + b)
        return 0

    lax.fori_loop(tiles // 2, tiles, attend, 0)

    @pl.when(half == 1)
    def _():
        settle(value_t.at[0:halo, 0:DIM], recv.at[7])

    lax.fori_loop(0, tiles // 2, attend, 0)

    settle(mixed, local.at[9])
    arrive(attended.at[:, pl.ds(0, (nb - 1) * DIM)], attended.at[:, columns_of(0)], 8)
    settle(fade_in.at[0 : n - 1], send.at[0])
    settle(state_in.at[0 : n - 1], send.at[1])
    settle(entering_in.at[0 : n - 1], send.at[3])
    for which in (2, 4, 6, 8):
        settle(value_out.at[0 : nb - 1], send.at[which])

    @pl.when(half == 0)
    def _():
        settle(value_out.at[0:halo], send.at[5])
        settle(value_out.at[0:halo], send.at[7])


def body(gla_query, gla_key, gla_value, log_gates, norm_gain, attn_query, attn_key, doc_blocks):
    n = lax.axis_size("ctx")
    nb = n // 2
    halo = nb // 2
    rows, columns = gla_query.shape
    out = jax.ShapeDtypeStruct((rows, columns), jnp.bfloat16)
    anywhere = pl.BlockSpec(memory_space=pl.ANY)
    vmem = pl.BlockSpec(memory_space=pltpu.VMEM)
    f32, bf16 = jnp.float32, jnp.bfloat16
    square = (BLOCK, DIM)
    tile = 2 * BLOCK
    steps = halo // 2 + 1
    return pl.pallas_call(
        functools.partial(kernel, n),
        out_shape=(out, out),
        in_specs=[pl.BlockSpec(memory_space=pltpu.SMEM), vmem, vmem] + [pl.BlockSpec(memory_space=pltpu.HBM)] * 5,
        out_specs=(anywhere, anywhere),
        scratch_shapes=[
            pltpu.VMEM((rows, columns), bf16),
            pltpu.VMEM((rows, columns), bf16),
            pltpu.VMEM((rows, columns), bf16),
            pltpu.VMEM((nb, *square), bf16),
            pltpu.VMEM((nb, *square), f32),
            pltpu.VMEM((nb, 1, BLOCK), f32),
            pltpu.VMEM((nb, 1, BLOCK), f32),
            pltpu.VMEM((n, 1, BLOCK), f32),
            pltpu.VMEM((nb, DIM, DIM), bf16),
            pltpu.VMEM((n, DIM // 2, DIM), bf16),
            pltpu.VMEM((n, DIM // 2, DIM), bf16),
            pltpu.VMEM((n, DIM // 2, DIM), bf16),
            pltpu.VMEM((nb, *square), f32),
            pltpu.VMEM((nb, *square), bf16),
            pltpu.VMEM((nb, *square), bf16),
            pltpu.VMEM((halo + nb, ROWS, BLOCK), bf16),
            pltpu.VMEM((halo + nb, *square), bf16),
            pltpu.VMEM((nb, *square), bf16),
            pltpu.VMEM((steps, tile, tile), f32),
            pltpu.VMEM((nb // 2, steps, tile, tile), bf16),
            pltpu.VMEM((nb, *square), bf16),
            pltpu.SemaphoreType.DMA((12,)),
            pltpu.SemaphoreType.DMA((12,)),
            pltpu.SemaphoreType.DMA((12,)),
            pltpu.SemaphoreType.DMA((nb,)),
        ],
        compiler_params=pltpu.CompilerParams(
            collective_id=0, has_side_effects=True, vmem_limit_bytes=50 * 2**20
        ),
    )(
        doc_blocks,
        norm_gain.reshape(nb, DIM),
        log_gates.T,
        gla_query,
        gla_key,
        gla_value,
        attn_query,
        attn_key,
    )


def solution(mesh):
    placed = P(("grp", "ctx"), None)
    return jax.shard_map(
        body,
        mesh=mesh,
        in_specs=(placed, placed, placed, placed, P(), placed, placed, P("grp")),
        out_specs=(placed, placed),
        check_vma=False,
    )
```

```python
import functools
import math

import jax
import jax.numpy as jnp
from jax import lax
from jax.experimental import pallas as pl
from jax.experimental.pallas import tpu as pltpu
from jax.sharding import PartitionSpec as P

BLOCK = 128
DIM = 128
LOW = -1e30
HIGH = 1e30
SCALE = DIM ** (-0.5)
TO_EXP2 = SCALE / math.log(2.0)
MESH = pl.DeviceIdType.MESH
NT = (((1,), (1,)), ((), ()))
ROWS = DIM + 16
STRIDE = 5
EARLY = 8


def columns_of(head):
    return pl.ds(pl.multiple_of(head * DIM, DIM), DIM)


def kernel(
    n,
    docs,
    gain,
    gates,
    gla_query,
    gla_key,
    gla_value,
    attn_query,
    attn_key,
    mixed,
    attended,
    own_query,
    own_key,
    own_value,
    own_value_t,
    gain_t,
    sums,
    fade_out,
    fade_in,
    state_out,
    state_in,
    entering_out,
    entering_in,
    inner,
    mixed_out,
    value_out,
    value_t,
    attn_key_in,
    attn_query_in,
    score_t,
    weights_t,
    attended_out,
    send,
    recv,
    local,
    recv_value,
):
    nb = n // 2
    halo = nb // 2
    part = DIM // 2
    place = lax.axis_index("ctx")
    half = lax.div(place, nb)
    rank = lax.rem(place, nb)
    base = half * nb
    turn = half * halo
    head = lax.rem(rank + turn, nb)
    partner = (1 - half) * nb + lax.rem(rank + halo, nb)
    barrier = pltpu.get_barrier_semaphore()

    def greet(i, _):
        pl.semaphore_signal(
            barrier, inc=1, device_id={"ctx": lax.rem(place + i, n)}, device_id_type=MESH
        )
        return 0

    lax.fori_loop(1, n, greet, 0)

    def push(src, dst, which, device):
        pltpu.make_async_remote_copy(
            src_ref=src,
            dst_ref=dst,
            send_sem=send.at[which],
            recv_sem=recv.at[which],
            device_id={"ctx": device},
            device_id_type=MESH,
        ).start()

    def push_any(src, dst, which, device):
        @pl.when(device != place)
        def _():
            push(src, dst, which, device)

        @pl.when(device == place)
        def _():
            pltpu.make_async_copy(src, dst, local.at[which]).start()

    def settle(ref, sem):
        pltpu.make_async_copy(ref, ref, sem).wait()

    def arrive(ref, one, which):
        settle(ref, recv.at[which])
        settle(one, local.at[which])

    pltpu.make_async_copy(gla_key, own_key, local.at[9]).start()
    pltpu.make_async_copy(gla_value, own_value, local.at[10]).start()
    pltpu.make_async_copy(gla_query, own_query, local.at[11]).start()

    pl.semaphore_wait(barrier, n - 1)

    def spread(src, dst, which):
        def one(i, _):
            h = lax.rem(head + STRIDE * i, nb)
            push(src.at[:, columns_of(h)], dst, which, base + lax.rem(rank + STRIDE * i, nb))
            return 0

        lax.fori_loop(1, nb, one, 0)
        pltpu.make_async_copy(src.at[:, columns_of(head)], dst, local.at[which]).start()

    spread(attn_key, attn_key_in.at[halo + rank], 2)

    lanes = lax.broadcasted_iota(jnp.int32, (BLOCK, BLOCK), 1)
    subs = lax.broadcasted_iota(jnp.int32, (BLOCK, BLOCK), 0)
    upto = jnp.where(subs <= lanes, 1.0, 0.0)
    summed = jnp.dot(
        gates[...], upto, precision=lax.Precision.HIGHEST, preferred_element_type=jnp.float32
    )
    for h in range(nb):
        sums[h] = summed[h : h + 1]
        fade_out[h] = jnp.exp(jnp.broadcast_to(summed[h : h + 1, BLOCK - 1 :], (1, BLOCK)))
    value_t[:, DIM:, :] = jnp.ones((value_t.shape[0], ROWS - DIM, BLOCK), jnp.bfloat16)

    @pl.when(half == 0)
    def _():
        attn_key_in[0:halo] = jnp.zeros((halo, BLOCK, DIM), jnp.bfloat16)
        value_t[0:halo, 0:DIM, :] = jnp.zeros((halo, DIM, BLOCK), jnp.bfloat16)

    def doc_start(block):
        start = jnp.int32(0)
        best = jnp.int32(0)
        for d in range(docs.shape[0]):
            best = jnp.where(start <= block, start, best)
            start = start + docs[d]
        return best

    settle(own_key, local.at[9])
    settle(own_value, local.at[10])

    def gained(i, _):
        for u in range(2):
            h = lax.rem(rank + STRIDE * (2 * i + u), nb)
            row = sums[h]
            tails = jnp.exp(row[:, BLOCK - 1 :] - row)
            turned = own_value[:, columns_of(h)].astype(jnp.float32).T
            own_value_t[h] = turned.astype(jnp.bfloat16)
            state = jnp.dot(
                (turned * tails).astype(jnp.bfloat16),
                own_key[:, columns_of(h)],
                preferred_element_type=jnp.float32,
            )
            state_out[h] = state.astype(jnp.bfloat16)
            for w in range(2):
                owner = h + w * nb
                push_any(fade_out.at[h], fade_in.at[place], 0, owner)
                push_any(
                    state_out.at[h, w * part : (w + 1) * part], state_in.at[place], 1, owner
                )
        return 0

    lax.fori_loop(0, nb // 2, gained, 0)
    @pl.when(lax.axis_index("grp") == 1)
    def _():
        spread(attn_query, attn_query_in.at[rank], 4)


    settle(own_query, local.at[11])
    causal = subs >= lanes

    def within(i, _):
        for u in range(2):
            h = 2 * i + u
            across = jnp.broadcast_to(sums[h], (BLOCK, BLOCK))
            down = across.T
            weight = jnp.where(
                causal, jnp.exp(jnp.where(causal, down - across, 0.0)), 0.0
            )
            scores = lax.dot_general(
                own_query[:, columns_of(h)],
                own_key[:, columns_of(h)],
                NT,
                preferred_element_type=jnp.float32,
            )
            inner[h] = lax.dot_general(
                own_value_t[h],
                (scores * (weight * SCALE)).astype(jnp.bfloat16),
                NT,
                preferred_element_type=jnp.float32,
            )
            gain_t[h] = jnp.broadcast_to(gain[pl.ds(h, 1), :], (BLOCK, DIM)).T
        return 0

    lax.fori_loop(0, nb // 2, within, 0)
    arrive(attn_key_in.at[halo : halo + nb - 1], attn_key_in.at[halo], 2)

    @pl.when(half == 0)
    def _():
        push(attn_key_in.at[nb : nb + halo], attn_key_in.at[0:halo], 5, partner)


    arrive(fade_in.at[0 : n - 1], fade_in.at[0], 0)
    arrive(state_in.at[0 : n - 1], state_in.at[0], 1)
    @pl.when(lax.axis_index("grp") == 0)
    def _():
        spread(attn_query, attn_query_in.at[rank], 4)


    def scan(i, state):
        for u in range(2):
            b = 2 * i + u
            state = state * jnp.where(doc_start(b) == b, 0.0, 1.0)
            entering_out[b] = state.astype(jnp.bfloat16)
            state = state * fade_in[b] + state_in[b].astype(jnp.float32)
        return state

    lax.fori_loop(0, nb, scan, jnp.zeros((part, DIM), jnp.float32))

    mine = entering_in.at[2 * rank + half]

    def enter(i, _):
        device = lax.rem(place + STRIDE * i, n)
        push(entering_out.at[device], mine, 3, device)
        return 0

    lax.fori_loop(1, n, enter, 0)
    pltpu.make_async_copy(entering_out.at[place], mine, local.at[3]).start()

    arrive(attn_query_in.at[0 : nb - 1], attn_query_in.at[0], 4)

    tile = 2 * BLOCK
    tiles = nb // 2
    steps = halo // 2 + 1
    tile_lanes = lax.broadcasted_iota(jnp.int32, (tile, tile), 1)
    tile_subs = lax.broadcasted_iota(jnp.int32, (tile, tile), 0)
    first_lanes = lax.broadcasted_iota(jnp.int32, (8, tile), 1) < BLOCK

    def weigh(k, _):
        i = lax.rem(k + tiles // 2, tiles)
        query = attn_query_in[pl.ds(2 * i, 2)].reshape(tile, DIM)
        first = base + 2 * i
        start = jnp.where(first_lanes, doc_start(first), doc_start(first + 1))
        peak = jnp.full((8, tile), LOW, jnp.float32)
        for j in range(steps):
            keys = attn_key_in[pl.ds(2 * (i + j), 2)].reshape(tile, DIM)
            scores = lax.dot_general(keys, query, NT, preferred_element_type=jnp.float32)
            if j == 0:
                scores = jnp.where(tile_subs > tile_lanes, scores, LOW)
            if j == steps - 1:
                scores = jnp.where(tile_subs <= tile_lanes, scores, LOW)
            score_t[j] = scores
            for u in range(2):
                block = first - halo + 2 * j + u
                top = jnp.max(
                    scores[u * BLOCK : (u + 1) * BLOCK].reshape(BLOCK // 8, 8, tile), axis=0
                )
                peak = jnp.maximum(peak, jnp.where(start <= block, top, LOW))
        peak = jnp.max(peak, axis=0, keepdims=True)
        for j in range(steps):
            for u in range(2):
                block = first - halo + 2 * j + u
                level = jnp.where(start[0:1] <= block, peak, HIGH)
                span = slice(u * BLOCK, (u + 1) * BLOCK)
                weights_t[i, j, span, :] = jnp.exp2(
                    (score_t[j, span, :] - level) * TO_EXP2
                ).astype(jnp.bfloat16)
        return 0

    lax.fori_loop(0, EARLY, weigh, 0)
    arrive(entering_in.at[0 : n - 1], entering_in.at[0], 3)

    def mix(i, _):
        for u in range(2):
            h = lax.rem(head + STRIDE * (2 * i + u), nb)
            entering = entering_in[pl.ds(2 * h, 2)].reshape(DIM, DIM)
            outer = lax.dot_general(
                entering,
                own_query[:, columns_of(h)],
                NT,
                preferred_element_type=jnp.float32,
            )
            total = inner[h] + (jnp.exp(sums[h]) * SCALE) * outer
            square = jnp.mean(total * total, axis=0, keepdims=True)
            value_out[h] = (total * lax.rsqrt(square + 1e-06) * gain_t[h]).astype(
                jnp.bfloat16
            )
            device = base + lax.rem(h + turn, nb)
            block = value_t.at[halo + rank, 0:DIM]

            @pl.when(device != place)
            def _():
                pltpu.make_async_remote_copy(
                    src_ref=value_out.at[h],
                    dst_ref=block,
                    send_sem=send.at[6],
                    recv_sem=recv_value.at[rank],
                    device_id={"ctx": device},
                    device_id_type=MESH,
                ).start()

            @pl.when(device == place)
            def _():
                pltpu.make_async_copy(value_out.at[h], block, local.at[6]).start()

        return 0

    lax.fori_loop(0, nb // 2, mix, 0)

    @pl.when(half == 1)
    def _():
        settle(attn_key_in.at[0:halo], recv.at[5])

    late = tiles - EARLY
    per_tile = nb // late

    def take(i):
        source = lax.rem(rank + nb - lax.rem(STRIDE * i, nb), nb)
        block = value_t.at[halo + source, 0:DIM]

        @pl.when(i == 0)
        def _():
            settle(block, local.at[6])

        @pl.when(i > 0)
        def _():
            settle(block, recv_value.at[source])

        @pl.when(jnp.logical_and(half == 0, source >= halo))
        def _():
            pltpu.make_async_remote_copy(
                src_ref=block,
                dst_ref=value_t.at[source - halo, 0:DIM],
                send_sem=send.at[7],
                recv_sem=recv.at[7],
                device_id={"ctx": partner},
                device_id_type=MESH,
            ).start()

    def weigh_and_take(k, _):
        weigh(EARLY + k, 0)
        for u in range(per_tile):
            h = k * per_tile + u
            mixed_out[h] = value_out[h].T
            pltpu.make_async_copy(
                mixed_out.at[h], mixed.at[:, columns_of(h)], local.at[9]
            ).start()
            take(h)
        return 0

    lax.fori_loop(0, late, weigh_and_take, 0)

    def attend(k, _):
        i = lax.div(k, tiles // 2) * (tiles // 2) + lax.rem(k + rank, tiles // 2)
        total = jnp.zeros((ROWS, tile), jnp.float32)
        for j in range(steps):
            at = 2 * (i + j)
            total = total + jnp.dot(
                jnp.concatenate([value_t[at], value_t[at + 1]], axis=1),
                weights_t[i, j],
                preferred_element_type=jnp.float32,
            )
        result = (total[0:DIM] / total[DIM : DIM + 1]).T.astype(jnp.bfloat16)
        for u in range(2):
            b = 2 * i + u
            attended_out[b] = result[u * BLOCK : (u + 1) * BLOCK]
            push_any(attended_out.at[b], attended.at[:, columns_of(head)], 8, base + b)
        return 0

    lax.fori_loop(tiles // 2, tiles, attend, 0)

    @pl.when(half == 1)
    def _():
        settle(value_t.at[0:halo, 0:DIM], recv.at[7])

    lax.fori_loop(0, tiles // 2, attend, 0)

    settle(mixed, local.at[9])
    arrive(attended.at[:, pl.ds(0, (nb - 1) * DIM)], attended.at[:, columns_of(0)], 8)
    settle(fade_in.at[0 : n - 1], send.at[0])
    settle(state_in.at[0 : n - 1], send.at[1])
    settle(entering_in.at[0 : n - 1], send.at[3])
    for which in (2, 4, 6, 8):
        settle(value_out.at[0 : nb - 1], send.at[which])

    @pl.when(half == 0)
    def _():
        settle(value_out.at[0:halo], send.at[5])
        settle(value_out.at[0:halo], send.at[7])


def body(gla_query, gla_key, gla_value, log_gates, norm_gain, attn_query, attn_key, doc_blocks):
    n = lax.axis_size("ctx")
    nb = n // 2
    halo = nb // 2
    rows, columns = gla_query.shape
    out = jax.ShapeDtypeStruct((rows, columns), jnp.bfloat16)
    anywhere = pl.BlockSpec(memory_space=pl.ANY)
    vmem = pl.BlockSpec(memory_space=pltpu.VMEM)
    f32, bf16 = jnp.float32, jnp.bfloat16
    square = (BLOCK, DIM)
    tile = 2 * BLOCK
    steps = halo // 2 + 1
    return pl.pallas_call(
        functools.partial(kernel, n),
        out_shape=(out, out),
        in_specs=[pl.BlockSpec(memory_space=pltpu.SMEM), vmem, vmem] + [pl.BlockSpec(memory_space=pltpu.HBM)] * 5,
        out_specs=(anywhere, anywhere),
        scratch_shapes=[
            pltpu.VMEM((rows, columns), bf16),
            pltpu.VMEM((rows, columns), bf16),
            pltpu.VMEM((rows, columns), bf16),
            pltpu.VMEM((nb, *square), bf16),
            pltpu.VMEM((nb, *square), f32),
            pltpu.VMEM((nb, 1, BLOCK), f32),
            pltpu.VMEM((nb, 1, BLOCK), f32),
            pltpu.VMEM((n, 1, BLOCK), f32),
            pltpu.VMEM((nb, DIM, DIM), bf16),
            pltpu.VMEM((n, DIM // 2, DIM), bf16),
            pltpu.VMEM((n, DIM // 2, DIM), bf16),
            pltpu.VMEM((n, DIM // 2, DIM), bf16),
            pltpu.VMEM((nb, *square), f32),
            pltpu.VMEM((nb, *square), bf16),
            pltpu.VMEM((nb, *square), bf16),
            pltpu.VMEM((halo + nb, ROWS, BLOCK), bf16),
            pltpu.VMEM((halo + nb, *square), bf16),
            pltpu.VMEM((nb, *square), bf16),
            pltpu.VMEM((steps, tile, tile), f32),
            pltpu.VMEM((nb // 2, steps, tile, tile), bf16),
            pltpu.VMEM((nb, *square), bf16),
            pltpu.SemaphoreType.DMA((12,)),
            pltpu.SemaphoreType.DMA((12,)),
            pltpu.SemaphoreType.DMA((12,)),
            pltpu.SemaphoreType.DMA((nb,)),
        ],
        compiler_params=pltpu.CompilerParams(
            collective_id=0, has_side_effects=True, vmem_limit_bytes=50 * 2**20
        ),
    )(
        doc_blocks,
        norm_gain.reshape(nb, DIM),
        log_gates.T,
        gla_query,
        gla_key,
        gla_value,
        attn_query,
        attn_key,
    )


def solution(mesh):
    placed = P(("grp", "ctx"), None)
    return jax.shard_map(
        body,
        mesh=mesh,
        in_specs=(placed, placed, placed, placed, P(), placed, placed, P("grp")),
        out_specs=(placed, placed),
        check_vma=False,
    )
```

```python
import functools
import math

import jax
import jax.numpy as jnp
from jax import lax
from jax.experimental import pallas as pl
from jax.experimental.pallas import tpu as pltpu
from jax.sharding import PartitionSpec as P

BLOCK = 128
DIM = 128
LOW = -1e30
HIGH = 1e30
SCALE = DIM ** (-0.5)
TO_EXP2 = SCALE / math.log(2.0)
MESH = pl.DeviceIdType.MESH
NT = (((1,), (1,)), ((), ()))
ROWS = DIM + 16
STRIDE = 5
EARLY = 8


def columns_of(head):
    return pl.ds(pl.multiple_of(head * DIM, DIM), DIM)


def kernel(
    n,
    docs,
    gain,
    gates,
    gla_query,
    gla_key,
    gla_value,
    attn_query,
    attn_key,
    mixed,
    attended,
    own_query,
    own_key,
    own_value,
    own_value_t,
    gain_t,
    sums,
    fade_out,
    fade_in,
    state_out,
    state_in,
    entering_out,
    entering_in,
    inner,
    mixed_out,
    value_out,
    value_t,
    attn_key_in,
    attn_query_in,
    score_t,
    weights_t,
    attended_out,
    send,
    recv,
    local,
    recv_value,
):
    nb = n // 2
    halo = nb // 2
    part = DIM // 2
    place = lax.axis_index("ctx")
    half = lax.div(place, nb)
    rank = lax.rem(place, nb)
    base = half * nb
    turn = half * halo
    head = lax.rem(rank + turn, nb)
    partner = (1 - half) * nb + lax.rem(rank + halo, nb)
    barrier = pltpu.get_barrier_semaphore()

    def greet(i, _):
        pl.semaphore_signal(
            barrier, inc=1, device_id={"ctx": lax.rem(place + i, n)}, device_id_type=MESH
        )
        return 0

    lax.fori_loop(1, n, greet, 0)

    def push(src, dst, which, device):
        pltpu.make_async_remote_copy(
            src_ref=src,
            dst_ref=dst,
            send_sem=send.at[which],
            recv_sem=recv.at[which],
            device_id={"ctx": device},
            device_id_type=MESH,
        ).start()

    def push_any(src, dst, which, device):
        @pl.when(device != place)
        def _():
            push(src, dst, which, device)

        @pl.when(device == place)
        def _():
            pltpu.make_async_copy(src, dst, local.at[which]).start()

    def settle(ref, sem):
        pltpu.make_async_copy(ref, ref, sem).wait()

    def arrive(ref, one, which):
        settle(ref, recv.at[which])
        settle(one, local.at[which])

    pltpu.make_async_copy(gla_key, own_key, local.at[9]).start()
    pltpu.make_async_copy(gla_value, own_value, local.at[10]).start()
    pltpu.make_async_copy(gla_query, own_query, local.at[11]).start()

    pl.semaphore_wait(barrier, n - 1)

    def spread(src, dst, which):
        def one(i, _):
            h = lax.rem(head + STRIDE * i, nb)
            push(src.at[:, columns_of(h)], dst, which, base + lax.rem(rank + STRIDE * i, nb))
            return 0

        lax.fori_loop(1, nb, one, 0)
        pltpu.make_async_copy(src.at[:, columns_of(head)], dst, local.at[which]).start()

    spread(attn_key, attn_key_in.at[halo + rank], 2)

    lanes = lax.broadcasted_iota(jnp.int32, (BLOCK, BLOCK), 1)
    subs = lax.broadcasted_iota(jnp.int32, (BLOCK, BLOCK), 0)
    upto = jnp.where(subs <= lanes, 1.0, 0.0)
    summed = jnp.dot(
        gates[...], upto, precision=lax.Precision.HIGHEST, preferred_element_type=jnp.float32
    )
    for h in range(nb):
        sums[h] = summed[h : h + 1]
        fade_out[h] = jnp.exp(jnp.broadcast_to(summed[h : h + 1, BLOCK - 1 :], (1, BLOCK)))
    value_t[:, DIM:, :] = jnp.ones((value_t.shape[0], ROWS - DIM, BLOCK), jnp.bfloat16)

    @pl.when(half == 0)
    def _():
        attn_key_in[0:halo] = jnp.zeros((halo, BLOCK, DIM), jnp.bfloat16)
        value_t[0:halo, 0:DIM, :] = jnp.zeros((halo, DIM, BLOCK), jnp.bfloat16)

    def doc_start(block):
        start = jnp.int32(0)
        best = jnp.int32(0)
        for d in range(docs.shape[0]):
            best = jnp.where(start <= block, start, best)
            start = start + docs[d]
        return best

    settle(own_key, local.at[9])
    settle(own_value, local.at[10])

    def gained(i, _):
        for u in range(2):
            h = lax.rem(rank + STRIDE * (2 * i + u), nb)
            row = sums[h]
            tails = jnp.exp(row[:, BLOCK - 1 :] - row)
            turned = own_value[:, columns_of(h)].astype(jnp.float32).T
            own_value_t[h] = turned.astype(jnp.bfloat16)
            state = jnp.dot(
                (turned * tails).astype(jnp.bfloat16),
                own_key[:, columns_of(h)],
                preferred_element_type=jnp.float32,
            )
            state_out[h] = state.astype(jnp.bfloat16)
            for w in range(2):
                owner = h + w * nb
                push_any(fade_out.at[h], fade_in.at[place], 0, owner)
                push_any(
                    state_out.at[h, w * part : (w + 1) * part], state_in.at[place], 1, owner
                )
        return 0

    lax.fori_loop(0, nb // 2, gained, 0)
    settle(own_query, local.at[11])
    causal = subs >= lanes

    def within(i, _):
        for u in range(2):
            h = 2 * i + u
            across = jnp.broadcast_to(sums[h], (BLOCK, BLOCK))
            down = across.T
            weight = jnp.where(
                causal, jnp.exp(jnp.where(causal, down - across, 0.0)), 0.0
            )
            scores = lax.dot_general(
                own_query[:, columns_of(h)],
                own_key[:, columns_of(h)],
                NT,
                preferred_element_type=jnp.float32,
            )
            inner[h] = lax.dot_general(
                own_value_t[h],
                (scores * (weight * SCALE)).astype(jnp.bfloat16),
                NT,
                preferred_element_type=jnp.float32,
            )
            gain_t[h] = jnp.broadcast_to(gain[pl.ds(h, 1), :], (BLOCK, DIM)).T
        return 0

    lax.fori_loop(0, nb // 2, within, 0)
    @pl.when(lax.axis_index("grp") == 1)
    def _():
        spread(attn_query, attn_query_in.at[rank], 4)

    arrive(attn_key_in.at[halo : halo + nb - 1], attn_key_in.at[halo], 2)

    @pl.when(half == 0)
    def _():
        push(attn_key_in.at[nb : nb + halo], attn_key_in.at[0:halo], 5, partner)


    arrive(fade_in.at[0 : n - 1], fade_in.at[0], 0)
    arrive(state_in.at[0 : n - 1], state_in.at[0], 1)
    @pl.when(lax.axis_index("grp") == 0)
    def _():
        spread(attn_query, attn_query_in.at[rank], 4)


    def scan(i, state):
        for u in range(2):
            b = 2 * i + u
            state = state * jnp.where(doc_start(b) == b, 0.0, 1.0)
            entering_out[b] = state.astype(jnp.bfloat16)
            state = state * fade_in[b] + state_in[b].astype(jnp.float32)
        return state

    lax.fori_loop(0, nb, scan, jnp.zeros((part, DIM), jnp.float32))

    mine = entering_in.at[2 * rank + half]

    def enter(i, _):
        device = lax.rem(place + STRIDE * i, n)
        push(entering_out.at[device], mine, 3, device)
        return 0

    lax.fori_loop(1, n, enter, 0)
    pltpu.make_async_copy(entering_out.at[place], mine, local.at[3]).start()

    arrive(attn_query_in.at[0 : nb - 1], attn_query_in.at[0], 4)

    tile = 2 * BLOCK
    tiles = nb // 2
    steps = halo // 2 + 1
    tile_lanes = lax.broadcasted_iota(jnp.int32, (tile, tile), 1)
    tile_subs = lax.broadcasted_iota(jnp.int32, (tile, tile), 0)
    first_lanes = lax.broadcasted_iota(jnp.int32, (8, tile), 1) < BLOCK

    def weigh(k, _):
        i = lax.rem(k + tiles // 2, tiles)
        query = attn_query_in[pl.ds(2 * i, 2)].reshape(tile, DIM)
        first = base + 2 * i
        start = jnp.where(first_lanes, doc_start(first), doc_start(first + 1))
        peak = jnp.full((8, tile), LOW, jnp.float32)
        for j in range(steps):
            keys = attn_key_in[pl.ds(2 * (i + j), 2)].reshape(tile, DIM)
            scores = lax.dot_general(keys, query, NT, preferred_element_type=jnp.float32)
            if j == 0:
                scores = jnp.where(tile_subs > tile_lanes, scores, LOW)
            if j == steps - 1:
                scores = jnp.where(tile_subs <= tile_lanes, scores, LOW)
            score_t[j] = scores
            for u in range(2):
                block = first - halo + 2 * j + u
                top = jnp.max(
                    scores[u * BLOCK : (u + 1) * BLOCK].reshape(BLOCK // 8, 8, tile), axis=0
                )
                peak = jnp.maximum(peak, jnp.where(start <= block, top, LOW))
        peak = jnp.max(peak, axis=0, keepdims=True)
        for j in range(steps):
            for u in range(2):
                block = first - halo + 2 * j + u
                level = jnp.where(start[0:1] <= block, peak, HIGH)
                span = slice(u * BLOCK, (u + 1) * BLOCK)
                weights_t[i, j, span, :] = jnp.exp2(
                    (score_t[j, span, :] - level) * TO_EXP2
                ).astype(jnp.bfloat16)
        return 0

    lax.fori_loop(0, EARLY, weigh, 0)
    arrive(entering_in.at[0 : n - 1], entering_in.at[0], 3)

    def mix(i, _):
        for u in range(2):
            h = lax.rem(head + STRIDE * (2 * i + u), nb)
            entering = entering_in[pl.ds(2 * h, 2)].reshape(DIM, DIM)
            outer = lax.dot_general(
                entering,
                own_query[:, columns_of(h)],
                NT,
                preferred_element_type=jnp.float32,
            )
            total = inner[h] + (jnp.exp(sums[h]) * SCALE) * outer
            square = jnp.mean(total * total, axis=0, keepdims=True)
            value_out[h] = (total * lax.rsqrt(square + 1e-06) * gain_t[h]).astype(
                jnp.bfloat16
            )
            device = base + lax.rem(h + turn, nb)
            block = value_t.at[halo + rank, 0:DIM]

            @pl.when(device != place)
            def _():
                pltpu.make_async_remote_copy(
                    src_ref=value_out.at[h],
                    dst_ref=block,
                    send_sem=send.at[6],
                    recv_sem=recv_value.at[rank],
                    device_id={"ctx": device},
                    device_id_type=MESH,
                ).start()

            @pl.when(device == place)
            def _():
                pltpu.make_async_copy(value_out.at[h], block, local.at[6]).start()

        return 0

    lax.fori_loop(0, nb // 2, mix, 0)

    @pl.when(half == 1)
    def _():
        settle(attn_key_in.at[0:halo], recv.at[5])

    late = tiles - EARLY
    per_tile = nb // late

    def take(i):
        source = lax.rem(rank + nb - lax.rem(STRIDE * i, nb), nb)
        block = value_t.at[halo + source, 0:DIM]

        @pl.when(i == 0)
        def _():
            settle(block, local.at[6])

        @pl.when(i > 0)
        def _():
            settle(block, recv_value.at[source])

        @pl.when(jnp.logical_and(half == 0, source >= halo))
        def _():
            pltpu.make_async_remote_copy(
                src_ref=block,
                dst_ref=value_t.at[source - halo, 0:DIM],
                send_sem=send.at[7],
                recv_sem=recv.at[7],
                device_id={"ctx": partner},
                device_id_type=MESH,
            ).start()

    def weigh_and_take(k, _):
        weigh(EARLY + k, 0)
        for u in range(per_tile):
            h = k * per_tile + u
            mixed_out[h] = value_out[h].T
            pltpu.make_async_copy(
                mixed_out.at[h], mixed.at[:, columns_of(h)], local.at[9]
            ).start()
            take(h)
        return 0

    lax.fori_loop(0, late, weigh_and_take, 0)

    def attend(k, _):
        i = lax.div(k, tiles // 2) * (tiles // 2) + lax.rem(k + rank, tiles // 2)
        total = jnp.zeros((ROWS, tile), jnp.float32)
        for j in range(steps):
            at = 2 * (i + j)
            total = total + jnp.dot(
                jnp.concatenate([value_t[at], value_t[at + 1]], axis=1),
                weights_t[i, j],
                preferred_element_type=jnp.float32,
            )
        result = (total[0:DIM] / total[DIM : DIM + 1]).T.astype(jnp.bfloat16)
        for u in range(2):
            b = 2 * i + u
            attended_out[b] = result[u * BLOCK : (u + 1) * BLOCK]
            push_any(attended_out.at[b], attended.at[:, columns_of(head)], 8, base + b)
        return 0

    lax.fori_loop(tiles // 2, tiles, attend, 0)

    @pl.when(half == 1)
    def _():
        settle(value_t.at[0:halo, 0:DIM], recv.at[7])

    lax.fori_loop(0, tiles // 2, attend, 0)

    settle(mixed, local.at[9])
    arrive(attended.at[:, pl.ds(0, (nb - 1) * DIM)], attended.at[:, columns_of(0)], 8)
    settle(fade_in.at[0 : n - 1], send.at[0])
    settle(state_in.at[0 : n - 1], send.at[1])
    settle(entering_in.at[0 : n - 1], send.at[3])
    for which in (2, 4, 6, 8):
        settle(value_out.at[0 : nb - 1], send.at[which])

    @pl.when(half == 0)
    def _():
        settle(value_out.at[0:halo], send.at[5])
        settle(value_out.at[0:halo], send.at[7])


def body(gla_query, gla_key, gla_value, log_gates, norm_gain, attn_query, attn_key, doc_blocks):
    n = lax.axis_size("ctx")
    nb = n // 2
    halo = nb // 2
    rows, columns = gla_query.shape
    out = jax.ShapeDtypeStruct((rows, columns), jnp.bfloat16)
    anywhere = pl.BlockSpec(memory_space=pl.ANY)
    vmem = pl.BlockSpec(memory_space=pltpu.VMEM)
    f32, bf16 = jnp.float32, jnp.bfloat16
    square = (BLOCK, DIM)
    tile = 2 * BLOCK
    steps = halo // 2 + 1
    return pl.pallas_call(
        functools.partial(kernel, n),
        out_shape=(out, out),
        in_specs=[pl.BlockSpec(memory_space=pltpu.SMEM), vmem, vmem] + [pl.BlockSpec(memory_space=pltpu.HBM)] * 5,
        out_specs=(anywhere, anywhere),
        scratch_shapes=[
            pltpu.VMEM((rows, columns), bf16),
            pltpu.VMEM((rows, columns), bf16),
            pltpu.VMEM((rows, columns), bf16),
            pltpu.VMEM((nb, *square), bf16),
            pltpu.VMEM((nb, *square), f32),
            pltpu.VMEM((nb, 1, BLOCK), f32),
            pltpu.VMEM((nb, 1, BLOCK), f32),
            pltpu.VMEM((n, 1, BLOCK), f32),
            pltpu.VMEM((nb, DIM, DIM), bf16),
            pltpu.VMEM((n, DIM // 2, DIM), bf16),
            pltpu.VMEM((n, DIM // 2, DIM), bf16),
            pltpu.VMEM((n, DIM // 2, DIM), bf16),
            pltpu.VMEM((nb, *square), f32),
            pltpu.VMEM((nb, *square), bf16),
            pltpu.VMEM((nb, *square), bf16),
            pltpu.VMEM((halo + nb, ROWS, BLOCK), bf16),
            pltpu.VMEM((halo + nb, *square), bf16),
            pltpu.VMEM((nb, *square), bf16),
            pltpu.VMEM((steps, tile, tile), f32),
            pltpu.VMEM((nb // 2, steps, tile, tile), bf16),
            pltpu.VMEM((nb, *square), bf16),
            pltpu.SemaphoreType.DMA((12,)),
            pltpu.SemaphoreType.DMA((12,)),
            pltpu.SemaphoreType.DMA((12,)),
            pltpu.SemaphoreType.DMA((nb,)),
        ],
        compiler_params=pltpu.CompilerParams(
            collective_id=0, has_side_effects=True, vmem_limit_bytes=50 * 2**20
        ),
    )(
        doc_blocks,
        norm_gain.reshape(nb, DIM),
        log_gates.T,
        gla_query,
        gla_key,
        gla_value,
        attn_query,
        attn_key,
    )


def solution(mesh):
    placed = P(("grp", "ctx"), None)
    return jax.shard_map(
        body,
        mesh=mesh,
        in_specs=(placed, placed, placed, placed, P(), placed, placed, P("grp")),
        out_specs=(placed, placed),
        check_vma=False,
    )
```

```python
import functools
import math

import jax
import jax.numpy as jnp
from jax import lax
from jax.experimental import pallas as pl
from jax.experimental.pallas import tpu as pltpu
from jax.sharding import PartitionSpec as P

BLOCK = 128
DIM = 128
LOW = -1e30
HIGH = 1e30
SCALE = DIM ** (-0.5)
TO_EXP2 = SCALE / math.log(2.0)
MESH = pl.DeviceIdType.MESH
NT = (((1,), (1,)), ((), ()))
ROWS = DIM + 16
STRIDE = 5
EARLY = 8


def columns_of(head):
    return pl.ds(pl.multiple_of(head * DIM, DIM), DIM)


def kernel(
    n,
    docs,
    gain,
    gates,
    gla_query,
    gla_key,
    gla_value,
    attn_query,
    attn_key,
    mixed,
    attended,
    own_query,
    own_key,
    own_value,
    own_value_t,
    gain_t,
    sums,
    fade_out,
    fade_in,
    state_out,
    state_in,
    entering_out,
    entering_in,
    inner,
    mixed_out,
    value_out,
    value_t,
    attn_key_in,
    attn_query_in,
    score_t,
    weights_t,
    attended_out,
    send,
    recv,
    local,
    recv_value,
):
    nb = n // 2
    halo = nb // 2
    part = DIM // 2
    place = lax.axis_index("ctx")
    half = lax.div(place, nb)
    rank = lax.rem(place, nb)
    base = half * nb
    turn = half * halo
    head = lax.rem(rank + turn, nb)
    partner = (1 - half) * nb + lax.rem(rank + halo, nb)
    barrier = pltpu.get_barrier_semaphore()

    def greet(i, _):
        pl.semaphore_signal(
            barrier, inc=1, device_id={"ctx": lax.rem(place + i, n)}, device_id_type=MESH
        )
        return 0

    lax.fori_loop(1, n, greet, 0)

    def push(src, dst, which, device):
        pltpu.make_async_remote_copy(
            src_ref=src,
            dst_ref=dst,
            send_sem=send.at[which],
            recv_sem=recv.at[which],
            device_id={"ctx": device},
            device_id_type=MESH,
        ).start()

    def push_any(src, dst, which, device):
        @pl.when(device != place)
        def _():
            push(src, dst, which, device)

        @pl.when(device == place)
        def _():
            pltpu.make_async_copy(src, dst, local.at[which]).start()

    def settle(ref, sem):
        pltpu.make_async_copy(ref, ref, sem).wait()

    def arrive(ref, one, which):
        settle(ref, recv.at[which])
        settle(one, local.at[which])

    pltpu.make_async_copy(gla_key, own_key, local.at[9]).start()
    pltpu.make_async_copy(gla_value, own_value, local.at[10]).start()
    pltpu.make_async_copy(gla_query, own_query, local.at[11]).start()

    pl.semaphore_wait(barrier, n - 1)

    def spread(src, dst, which):
        def one(i, _):
            h = lax.rem(head + STRIDE * i, nb)
            push(src.at[:, columns_of(h)], dst, which, base + lax.rem(rank + STRIDE * i, nb))
            return 0

        lax.fori_loop(1, nb, one, 0)
        pltpu.make_async_copy(src.at[:, columns_of(head)], dst, local.at[which]).start()

    spread(attn_key, attn_key_in.at[halo + rank], 2)

    lanes = lax.broadcasted_iota(jnp.int32, (BLOCK, BLOCK), 1)
    subs = lax.broadcasted_iota(jnp.int32, (BLOCK, BLOCK), 0)
    upto = jnp.where(subs <= lanes, 1.0, 0.0)
    summed = jnp.dot(
        gates[...], upto, precision=lax.Precision.HIGHEST, preferred_element_type=jnp.float32
    )
    for h in range(nb):
        sums[h] = summed[h : h + 1]
        fade_out[h] = jnp.exp(jnp.broadcast_to(summed[h : h + 1, BLOCK - 1 :], (1, BLOCK)))
    value_t[:, DIM:, :] = jnp.ones((value_t.shape[0], ROWS - DIM, BLOCK), jnp.bfloat16)

    @pl.when(half == 0)
    def _():
        attn_key_in[0:halo] = jnp.zeros((halo, BLOCK, DIM), jnp.bfloat16)
        value_t[0:halo, 0:DIM, :] = jnp.zeros((halo, DIM, BLOCK), jnp.bfloat16)

    def doc_start(block):
        start = jnp.int32(0)
        best = jnp.int32(0)
        for d in range(docs.shape[0]):
            best = jnp.where(start <= block, start, best)
            start = start + docs[d]
        return best

    settle(own_key, local.at[9])
    settle(own_value, local.at[10])

    def gained(i, _):
        for u in range(2):
            h = lax.rem(rank + STRIDE * (2 * i + u), nb)
            row = sums[h]
            tails = jnp.exp(row[:, BLOCK - 1 :] - row)
            turned = own_value[:, columns_of(h)].astype(jnp.float32).T
            own_value_t[h] = turned.astype(jnp.bfloat16)
            state = jnp.dot(
                (turned * tails).astype(jnp.bfloat16),
                own_key[:, columns_of(h)],
                preferred_element_type=jnp.float32,
            )
            state_out[h] = state.astype(jnp.bfloat16)
            for w in range(2):
                owner = h + w * nb
                push_any(fade_out.at[h], fade_in.at[place], 0, owner)
                push_any(
                    state_out.at[h, w * part : (w + 1) * part], state_in.at[place], 1, owner
                )
        return 0

    lax.fori_loop(0, nb // 2, gained, 0)
    settle(own_query, local.at[11])
    causal = subs >= lanes

    def within(i, _):
        for u in range(2):
            h = 2 * i + u
            across = jnp.broadcast_to(sums[h], (BLOCK, BLOCK))
            down = across.T
            weight = jnp.where(
                causal, jnp.exp(jnp.where(causal, down - across, 0.0)), 0.0
            )
            scores = lax.dot_general(
                own_query[:, columns_of(h)],
                own_key[:, columns_of(h)],
                NT,
                preferred_element_type=jnp.float32,
            )
            inner[h] = lax.dot_general(
                own_value_t[h],
                (scores * (weight * SCALE)).astype(jnp.bfloat16),
                NT,
                preferred_element_type=jnp.float32,
            )
            gain_t[h] = jnp.broadcast_to(gain[pl.ds(h, 1), :], (BLOCK, DIM)).T
        return 0

    lax.fori_loop(0, nb // 2, within, 0)
    @pl.when(lax.axis_index("grp") == 1)
    def _():
        spread(attn_query, attn_query_in.at[rank], 4)

    arrive(attn_key_in.at[halo : halo + nb - 1], attn_key_in.at[halo], 2)


    arrive(fade_in.at[0 : n - 1], fade_in.at[0], 0)
    arrive(state_in.at[0 : n - 1], state_in.at[0], 1)
    @pl.when(lax.axis_index("grp") == 0)
    def _():
        spread(attn_query, attn_query_in.at[rank], 4)


    def scan(i, state):
        for u in range(2):
            b = 2 * i + u
            state = state * jnp.where(doc_start(b) == b, 0.0, 1.0)
            entering_out[b] = state.astype(jnp.bfloat16)
            state = state * fade_in[b] + state_in[b].astype(jnp.float32)
        return state

    lax.fori_loop(0, nb, scan, jnp.zeros((part, DIM), jnp.float32))

    mine = entering_in.at[2 * rank + half]

    def enter(i, _):
        device = lax.rem(place + STRIDE * i, n)
        push(entering_out.at[device], mine, 3, device)
        return 0

    lax.fori_loop(1, n, enter, 0)
    pltpu.make_async_copy(entering_out.at[place], mine, local.at[3]).start()

    @pl.when(half == 0)
    def _():
        push(attn_key_in.at[nb : nb + halo], attn_key_in.at[0:halo], 5, partner)


    arrive(attn_query_in.at[0 : nb - 1], attn_query_in.at[0], 4)

    tile = 2 * BLOCK
    tiles = nb // 2
    steps = halo // 2 + 1
    tile_lanes = lax.broadcasted_iota(jnp.int32, (tile, tile), 1)
    tile_subs = lax.broadcasted_iota(jnp.int32, (tile, tile), 0)
    first_lanes = lax.broadcasted_iota(jnp.int32, (8, tile), 1) < BLOCK

    def weigh(k, _):
        i = lax.rem(k + tiles // 2, tiles)
        query = attn_query_in[pl.ds(2 * i, 2)].reshape(tile, DIM)
        first = base + 2 * i
        start = jnp.where(first_lanes, doc_start(first), doc_start(first + 1))
        peak = jnp.full((8, tile), LOW, jnp.float32)
        for j in range(steps):
            keys = attn_key_in[pl.ds(2 * (i + j), 2)].reshape(tile, DIM)
            scores = lax.dot_general(keys, query, NT, preferred_element_type=jnp.float32)
            if j == 0:
                scores = jnp.where(tile_subs > tile_lanes, scores, LOW)
            if j == steps - 1:
                scores = jnp.where(tile_subs <= tile_lanes, scores, LOW)
            score_t[j] = scores
            for u in range(2):
                block = first - halo + 2 * j + u
                top = jnp.max(
                    scores[u * BLOCK : (u + 1) * BLOCK].reshape(BLOCK // 8, 8, tile), axis=0
                )
                peak = jnp.maximum(peak, jnp.where(start <= block, top, LOW))
        peak = jnp.max(peak, axis=0, keepdims=True)
        for j in range(steps):
            for u in range(2):
                block = first - halo + 2 * j + u
                level = jnp.where(start[0:1] <= block, peak, HIGH)
                span = slice(u * BLOCK, (u + 1) * BLOCK)
                weights_t[i, j, span, :] = jnp.exp2(
                    (score_t[j, span, :] - level) * TO_EXP2
                ).astype(jnp.bfloat16)
        return 0

    lax.fori_loop(0, EARLY, weigh, 0)
    arrive(entering_in.at[0 : n - 1], entering_in.at[0], 3)

    def mix(i, _):
        for u in range(2):
            h = lax.rem(head + STRIDE * (2 * i + u), nb)
            entering = entering_in[pl.ds(2 * h, 2)].reshape(DIM, DIM)
            outer = lax.dot_general(
                entering,
                own_query[:, columns_of(h)],
                NT,
                preferred_element_type=jnp.float32,
            )
            total = inner[h] + (jnp.exp(sums[h]) * SCALE) * outer
            square = jnp.mean(total * total, axis=0, keepdims=True)
            value_out[h] = (total * lax.rsqrt(square + 1e-06) * gain_t[h]).astype(
                jnp.bfloat16
            )
            device = base + lax.rem(h + turn, nb)
            block = value_t.at[halo + rank, 0:DIM]

            @pl.when(device != place)
            def _():
                pltpu.make_async_remote_copy(
                    src_ref=value_out.at[h],
                    dst_ref=block,
                    send_sem=send.at[6],
                    recv_sem=recv_value.at[rank],
                    device_id={"ctx": device},
                    device_id_type=MESH,
                ).start()

            @pl.when(device == place)
            def _():
                pltpu.make_async_copy(value_out.at[h], block, local.at[6]).start()

        return 0

    lax.fori_loop(0, nb // 2, mix, 0)

    @pl.when(half == 1)
    def _():
        settle(attn_key_in.at[0:halo], recv.at[5])

    late = tiles - EARLY
    per_tile = nb // late

    def take(i):
        source = lax.rem(rank + nb - lax.rem(STRIDE * i, nb), nb)
        block = value_t.at[halo + source, 0:DIM]

        @pl.when(i == 0)
        def _():
            settle(block, local.at[6])

        @pl.when(i > 0)
        def _():
            settle(block, recv_value.at[source])

        @pl.when(jnp.logical_and(half == 0, source >= halo))
        def _():
            pltpu.make_async_remote_copy(
                src_ref=block,
                dst_ref=value_t.at[source - halo, 0:DIM],
                send_sem=send.at[7],
                recv_sem=recv.at[7],
                device_id={"ctx": partner},
                device_id_type=MESH,
            ).start()

    def weigh_and_take(k, _):
        weigh(EARLY + k, 0)
        for u in range(per_tile):
            h = k * per_tile + u
            mixed_out[h] = value_out[h].T
            pltpu.make_async_copy(
                mixed_out.at[h], mixed.at[:, columns_of(h)], local.at[9]
            ).start()
            take(h)
        return 0

    lax.fori_loop(0, late, weigh_and_take, 0)

    def attend(k, _):
        i = lax.div(k, tiles // 2) * (tiles // 2) + lax.rem(k + rank, tiles // 2)
        total = jnp.zeros((ROWS, tile), jnp.float32)
        for j in range(steps):
            at = 2 * (i + j)
            total = total + jnp.dot(
                jnp.concatenate([value_t[at], value_t[at + 1]], axis=1),
                weights_t[i, j],
                preferred_element_type=jnp.float32,
            )
        result = (total[0:DIM] / total[DIM : DIM + 1]).T.astype(jnp.bfloat16)
        for u in range(2):
            b = 2 * i + u
            attended_out[b] = result[u * BLOCK : (u + 1) * BLOCK]
            push_any(attended_out.at[b], attended.at[:, columns_of(head)], 8, base + b)
        return 0

    lax.fori_loop(tiles // 2, tiles, attend, 0)

    @pl.when(half == 1)
    def _():
        settle(value_t.at[0:halo, 0:DIM], recv.at[7])

    lax.fori_loop(0, tiles // 2, attend, 0)

    settle(mixed, local.at[9])
    arrive(attended.at[:, pl.ds(0, (nb - 1) * DIM)], attended.at[:, columns_of(0)], 8)
    settle(fade_in.at[0 : n - 1], send.at[0])
    settle(state_in.at[0 : n - 1], send.at[1])
    settle(entering_in.at[0 : n - 1], send.at[3])
    for which in (2, 4, 6, 8):
        settle(value_out.at[0 : nb - 1], send.at[which])

    @pl.when(half == 0)
    def _():
        settle(value_out.at[0:halo], send.at[5])
        settle(value_out.at[0:halo], send.at[7])


def body(gla_query, gla_key, gla_value, log_gates, norm_gain, attn_query, attn_key, doc_blocks):
    n = lax.axis_size("ctx")
    nb = n // 2
    halo = nb // 2
    rows, columns = gla_query.shape
    out = jax.ShapeDtypeStruct((rows, columns), jnp.bfloat16)
    anywhere = pl.BlockSpec(memory_space=pl.ANY)
    vmem = pl.BlockSpec(memory_space=pltpu.VMEM)
    f32, bf16 = jnp.float32, jnp.bfloat16
    square = (BLOCK, DIM)
    tile = 2 * BLOCK
    steps = halo // 2 + 1
    return pl.pallas_call(
        functools.partial(kernel, n),
        out_shape=(out, out),
        in_specs=[pl.BlockSpec(memory_space=pltpu.SMEM), vmem, vmem] + [pl.BlockSpec(memory_space=pltpu.HBM)] * 5,
        out_specs=(anywhere, anywhere),
        scratch_shapes=[
            pltpu.VMEM((rows, columns), bf16),
            pltpu.VMEM((rows, columns), bf16),
            pltpu.VMEM((rows, columns), bf16),
            pltpu.VMEM((nb, *square), bf16),
            pltpu.VMEM((nb, *square), f32),
            pltpu.VMEM((nb, 1, BLOCK), f32),
            pltpu.VMEM((nb, 1, BLOCK), f32),
            pltpu.VMEM((n, 1, BLOCK), f32),
            pltpu.VMEM((nb, DIM, DIM), bf16),
            pltpu.VMEM((n, DIM // 2, DIM), bf16),
            pltpu.VMEM((n, DIM // 2, DIM), bf16),
            pltpu.VMEM((n, DIM // 2, DIM), bf16),
            pltpu.VMEM((nb, *square), f32),
            pltpu.VMEM((nb, *square), bf16),
            pltpu.VMEM((nb, *square), bf16),
            pltpu.VMEM((halo + nb, ROWS, BLOCK), bf16),
            pltpu.VMEM((halo + nb, *square), bf16),
            pltpu.VMEM((nb, *square), bf16),
            pltpu.VMEM((steps, tile, tile), f32),
            pltpu.VMEM((nb // 2, steps, tile, tile), bf16),
            pltpu.VMEM((nb, *square), bf16),
            pltpu.SemaphoreType.DMA((12,)),
            pltpu.SemaphoreType.DMA((12,)),
            pltpu.SemaphoreType.DMA((12,)),
            pltpu.SemaphoreType.DMA((nb,)),
        ],
        compiler_params=pltpu.CompilerParams(
            collective_id=0, has_side_effects=True, vmem_limit_bytes=50 * 2**20
        ),
    )(
        doc_blocks,
        norm_gain.reshape(nb, DIM),
        log_gates.T,
        gla_query,
        gla_key,
        gla_value,
        attn_query,
        attn_key,
    )


def solution(mesh):
    placed = P(("grp", "ctx"), None)
    return jax.shard_map(
        body,
        mesh=mesh,
        in_specs=(placed, placed, placed, placed, P(), placed, placed, P("grp")),
        out_specs=(placed, placed),
        check_vma=False,
    )
```
